256 devices in a mesh: row: 8 (over x, core), col: 32 (over y, z).
Axes of the slice: x: 4, y: 4, z: 8, core: 2. Of those that a mesh axis runs over, the one named last changes fastest.
Arguments:
- tokens: bfloat16 [4096, 6144], P('row', 'col')
- ln_gain: bfloat16 [6144], P('col'), may hold values from 0.5 to 1.5
- q_weight: bfloat16 [6144, 4096], P('row', 'col'), may hold values from -0.078125 to 0.078125
- k_weight: bfloat16 [6144, 4096], P('row', 'col'), may hold values from -0.078125 to 0.078125
- v_weight: bfloat16 [6144, 4096], P('row', 'col'), may hold values from -0.078125 to 0.078125
- up_weight: bfloat16 [6144, 12288], P('row', 'col'), may hold values from -0.078125 to 0.078125
- out_weight: bfloat16 [4096, 6144], P('row', 'col'), may hold values from -0.375 to 0.375
- down_weight: bfloat16 [12288, 6144], P('row', 'col'), may hold values from -0.0546875 to 0.0546875
- q_gain: float32 [32, 128], P('col'), may hold values from 0.5 to 9, as said below
- k_gain: float32 [32, 128], P('col'), may hold values from 0.5 to 9, as said below
Outputs:
- mixed: bfloat16 [4096, 6144], P('row', 'col')
The draws below stay inside these ranges and needn't reach their ends.
Inputs may be any that keep to these rules, and one draw needn't show every extreme that they name: `q_gain`: positive gains. `k_gain`: positive gains.
All inputs are finite; a program needn't handle non-finite values.
Results may differ from the reference program's by a relative error of at most 0.008.
The reference program's roundings to bfloat16 on the way (of `normed`, `probs`, `attended` and `hidden`) count: a program that leaves them out, or rounds other values in their place, can miss the bound.
Values may be sent and summed in bfloat16 or wider, within the bound.
No kernel may reach another device: no remote copies, remote signals or barrier semaphores. Data moves between devices by JAX's collectives and lax.ppermute only.
A program may use at most 128 MiB of HBM per device.

```python
import math
import jax
import jax.numpy as jnp
from jax import lax

D = 6144
FF = 12288
HD = 128
HEADS = 32
TOKENS = 4096


def draw_tokens(key, part):
    key = jax.random.fold_in(key, 11)
    first_key, second_key, third_key = jax.random.split(key, 3)
    row_scale = jnp.exp(jax.random.uniform(first_key, (TOKENS, 1), jnp.float32, math.log(0.3), math.log(3.0)))
    rising = jnp.exp(jnp.linspace(math.log(0.5), math.log(2.0), D).astype(jnp.float32))
    rough = jax.random.uniform(second_key, (D,), jnp.float32, 0.7, 1.4)
    col_scale = (rising * rough)[None, :]
    base = jax.random.normal(third_key, (TOKENS, D), jnp.float32)
    return (base * row_scale * col_scale).astype(jnp.bfloat16)


def draw_q_gain(key, part):
    key = jax.random.fold_in(key, 21)
    values = jax.random.uniform(key, (HEADS, HD), jnp.float32, 0.5, 2.0)
    return values


def draw_k_gain(key, part):
    key = jax.random.fold_in(key, 31)
    values = jax.random.uniform(key, (HEADS, HD), jnp.float32, 0.5, 2.0)
    return values


def block_levels(rng, dims, shards, low, top_value):
    level, own = 1.0, jax.random.fold_in(rng, 6)
    for dim, parts in shards:
        steps = jnp.exp(jax.random.uniform(jax.random.fold_in(own, dim), (parts,), jnp.float32, low / len(shards), top_value / len(shards)))
        level = level * jnp.repeat(steps, dims[dim] // parts).reshape([-1 if axis == dim else 1 for axis in range(len(dims))])
    return level


def scatter_about(key, shape, width, reach, shards=(), kind=jnp.bfloat16):
    factor_of = block_levels(key, shape, shards, -0.22, 0.18) if shards else 1.0
    values = jax.random.normal(key, shape, jnp.float32) * width * factor_of
    return jnp.minimum(jnp.maximum(values, -reach), reach).astype(kind)


def setup_inputs(seed: int = 0) -> dict:
    splits = jax.random.split(jax.random.key(seed), 11)
    return {
        "tokens": draw_tokens(jax.random.fold_in(splits[10], 71), 0),
        "ln_gain": jnp.clip(0.5 + 1.0 * jax.random.uniform(splits[1], (D,), jnp.float32) ** block_levels(splits[1], (D,), ((0, 32),), -0.2, 0.2), 0.5, 1.5).astype(jnp.bfloat16),
        "q_weight": scatter_about(splits[2], (D, HEADS * HD), D ** -0.5, 0.078125, ((0, 8), (1, 32))),
        "k_weight": scatter_about(splits[3], (D, HEADS * HD), D ** -0.5, 0.078125, ((0, 8), (1, 32))),
        "v_weight": scatter_about(splits[4], (D, HEADS * HD), D ** -0.5, 0.078125, ((0, 8), (1, 32))),
        "up_weight": scatter_about(splits[5], (D, FF), D ** -0.5, 0.078125, ((0, 8), (1, 32))),
        "out_weight": scatter_about(splits[6], (HEADS * HD, D), (HEADS * HD // 16) ** -0.5, 0.375, ((0, 8), (1, 32))),
        "down_weight": scatter_about(splits[7], (FF, D), FF ** -0.5, 0.0546875, ((0, 8), (1, 32))),
        "q_gain": draw_q_gain(jax.random.fold_in(splits[10], 71), 0),
        "k_gain": draw_k_gain(jax.random.fold_in(splits[10], 71), 0),
    }


epsilon = 1e-06

def normalize(values, gain):
    average = lax.optimization_barrier(jnp.mean(values, axis=-1, keepdims=True))
    variance = lax.optimization_barrier(jnp.mean(values * values, axis=-1, keepdims=True)) - average * average
    return (values - average) * lax.rsqrt(variance + epsilon) * gain

def attend(operands):
    query_head, key_head, value_head = operands
    scores = jnp.dot(query_head, key_head.T, preferred_element_type=jnp.float32) * (1.0 / math.sqrt(HD))
    largest = lax.optimization_barrier(jnp.max(scores, axis=-1, keepdims=True))
    exponent = jnp.exp(scores - largest)
    probs = (exponent / lax.optimization_barrier(jnp.sum(exponent, axis=-1, keepdims=True))).astype(jnp.bfloat16)
    return jnp.dot(probs, value_head, preferred_element_type=jnp.float32).astype(jnp.bfloat16)

def reference(tokens, ln_gain, q_weight, k_weight, v_weight, up_weight, out_weight, down_weight, q_gain, k_gain):
    floats = tokens.astype(jnp.float32)
    normed = normalize(floats, ln_gain.astype(jnp.float32)).astype(jnp.bfloat16)
    queries = jnp.dot(normed, q_weight, preferred_element_type=jnp.float32)
    key_rows = jnp.dot(normed, k_weight, preferred_element_type=jnp.float32)
    value_rows = jnp.dot(normed, v_weight, preferred_element_type=jnp.float32)
    up_part = jnp.dot(normed, up_weight, preferred_element_type=jnp.float32)
    query_norm = normalize(queries.reshape(TOKENS, HEADS, HD), q_gain).astype(jnp.bfloat16)
    key_norm = normalize(key_rows.reshape(TOKENS, HEADS, HD), k_gain).astype(jnp.bfloat16)
    value_bf = value_rows.astype(jnp.bfloat16).reshape(TOKENS, HEADS, HD)
    per_head = lax.map(attend, (query_norm.transpose(1, 0, 2), key_norm.transpose(1, 0, 2), value_bf.transpose(1, 0, 2)))
    attended = per_head.transpose(1, 0, 2).reshape(TOKENS, HEADS * HD)
    hidden = jax.nn.gelu(up_part).astype(jnp.bfloat16)
    summed = floats + jnp.dot(attended, out_weight, preferred_element_type=jnp.float32)
    summed = summed + jnp.dot(hidden, down_weight, preferred_element_type=jnp.float32)
    return summed.astype(jnp.bfloat16)
```

```python
import math

import jax
import jax.numpy as jnp
from jax import lax
from jax.experimental import pallas as pl
from jax.experimental.pallas import tpu as pltpu
from jax.sharding import PartitionSpec as P

D = 6144
HD = 128
NX, NY, NZ = 4, 4, 8
ROWS = 2 * NX
M = 512
BLOCK = D // (NY * NZ)
FIRST = 80
GAIN_ROWS = 16
PART1 = FIRST + GAIN_ROWS
PART2 = BLOCK - FIRST
DEEP = D // ROWS
FFL = 384
KV = 2 * HD
QU = HD + FFL
OUT_K = 512
DOWN_K = 1536
Y_OFF = (0, 1, 3, 2)
Z_OFF = (0, 1, 7, 2, 6, 3, 5, 4)
epsilon = 1e-06
f32, bf16 = jnp.float32, jnp.bfloat16
VMEM_LIMIT = 56 * 1024 * 1024
ANY = pl.BlockSpec(memory_space=pl.ANY)
VMEM = pl.BlockSpec(memory_space=pltpu.VMEM)


def along_col(value, dy, dz):
    pairs = [
        (y * NZ + z, ((y + dy) % NY) * NZ + (z + dz) % NZ) for y in range(NY) for z in range(NZ)
    ]
    return lax.ppermute(value, "col", pairs)


def along_row(value, dx, dc):
    pairs = [
        (x * 2 + c, ((x + dx) % NX) * 2 + (c + dc) % 2) for x in range(NX) for c in range(2)
    ]
    return lax.ppermute(value, "row", pairs)


def z_ring(block, half=None):
    forth = back = block
    blocks = [block]
    for _ in range(3):
        forth, back = along_col(forth, 0, 1), along_col(back, 0, -1)
        blocks += [forth, back]
    if half is None:
        return blocks + [along_col(forth, 0, 1)]
    return blocks + [along_col(forth[:half], 0, 1), along_col(back[half:], 0, -1)]


def position():
    col = lax.axis_index("col")
    return lax.div(col, NZ), lax.rem(col, NZ)


def back_from(index, offset, size):
    return lax.rem(index + (size - offset), size)


def start_all(copies, sems):
    started = []
    for number, (source, target) in enumerate(copies):
        copy = pltpu.make_async_copy(source, target, sems.at[number])
        copy.start()
        started.append(copy)
    return started


def head_norm(values, gain):
    average = jnp.mean(values, axis=0, keepdims=True)
    variance = jnp.mean(values * values, axis=0, keepdims=True) - average * average
    return (values - average) * lax.rsqrt(variance + epsilon) * gain


def piece_rows(refs, rows):
    spans = [(ref, place, 0, rows) for place, ref in enumerate(refs[:7])]
    if len(refs) == 8:
        return spans + [(refs[7], 7, 0, rows)]
    half = refs[7].shape[0]
    return spans + [(refs[7], 7, 0, half), (refs[8], 7, half, rows - half)]


def norm_kv_kernel(*refs):
    first, second = refs[:9], refs[9:14]
    weights, k_gain, normed_out, kv_out = refs[14:18]
    held, gains, gain_wide, w_held, sums, sems, out_sems = refs[18:]
    y, z = position()
    copies = []
    for ref, place, begin, rows in piece_rows(first, NY * PART1):
        z_from = back_from(z, Z_OFF[place], NZ)
        for sub in range(rows // PART1):
            y_from = back_from(y, Y_OFF[begin // PART1 + sub], NY)
            block = y_from * NZ + z_from
            row = pl.multiple_of(block * BLOCK, 16)
            copies.append((ref.at[pl.ds(sub * PART1, FIRST)], held.at[pl.ds(row, FIRST)]))
            row = pl.multiple_of(block * GAIN_ROWS, 16)
            copies.append(
                (ref.at[pl.ds(sub * PART1 + FIRST, GAIN_ROWS)], gains.at[pl.ds(row, GAIN_ROWS)])
            )
    spans = [(second[0], 0, 0, 8), (second[1], 1, 0, 8), (second[2], 2, 0, 8)]
    spans += [(second[3], 3, 0, 4), (second[4], 3, 4, 4)]
    for ref, place, begin, count in spans:
        y_from = back_from(y, Y_OFF[place], NY)
        for sub in range(count):
            z_from = back_from(z, Z_OFF[begin + sub], NZ)
            row = pl.multiple_of((y_from * NZ + z_from) * BLOCK + FIRST, 16)
            copies.append((ref.at[pl.ds(sub * PART2, PART2)], held.at[pl.ds(row, PART2)]))
    for part in range(ROWS):
        copies.append((weights.at[part, pl.ds(0, KV)], w_held.at[part]))
    started = start_all(copies, sems)
    for copy in started[:-ROWS]:
        copy.wait()

    gain_rows = jnp.max(gains[:, :256].astype(f32).reshape(NY * NZ, GAIN_ROWS, 256), axis=1)
    gain_columns = gain_rows.T
    for block in range(NY * NZ):
        gain_wide[block * BLOCK : (block + 1) * BLOCK, :] = jnp.broadcast_to(
            gain_columns[:BLOCK, block : block + 1], (BLOCK, 128)
        )

    chunk = 96

    def add(step, totals):
        rows = held[pl.ds(pl.multiple_of(step * chunk, chunk), chunk), :].astype(f32)
        rows = rows.reshape(chunk // 8, 8, M)
        return totals[0] + jnp.sum(rows, axis=0), totals[1] + jnp.sum(rows * rows, axis=0)

    zero = jnp.zeros((8, M), f32)
    totals = lax.fori_loop(0, D // chunk, add, (zero, zero))
    average = jnp.sum(totals[0], axis=0, keepdims=True) / D
    variance = jnp.sum(totals[1], axis=0, keepdims=True) / D - average * average
    scale = lax.rsqrt(variance + epsilon)
    for copy in started[-ROWS:]:
        copy.wait()
    sums[...] = jnp.zeros_like(sums)

    def project(part, _):
        def norm(step, _):
            where = pl.ds(pl.multiple_of(part * DEEP + step * chunk, chunk), chunk)
            gain = jnp.concatenate([gain_wide[where, :]] * 4, axis=1)
            rows = held[where, :].astype(f32)
            held[where, :] = ((rows - average) * scale * gain).astype(bf16)
            return 0

        lax.fori_loop(0, DEEP // chunk, norm, 0)
        where = pl.ds(pl.multiple_of(part * DEEP, DEEP), DEEP)
        pltpu.make_async_copy(held.at[where], normed_out.at[where], out_sems.at[part]).start()
        sums[...] += jnp.dot(w_held[part], held[where, :], preferred_element_type=f32)
        return 0

    lax.fori_loop(0, ROWS, project, 0)
    kv_out[:HD, :] = head_norm(sums[:HD, :], k_gain[...]).astype(bf16)
    kv_out[HD:, :] = sums[HD:, :].astype(bf16)
    for part in range(ROWS):
        where = pl.ds(part * DEEP, DEEP)
        pltpu.make_async_copy(held.at[where], normed_out.at[where], out_sems.at[part]).wait()


def norm_kv(first, second, weights, k_gain):
    copies = 64 + 32 + ROWS
    return pl.pallas_call(
        norm_kv_kernel,
        out_shape=(jax.ShapeDtypeStruct((D, M), bf16), jax.ShapeDtypeStruct((KV, M), bf16)),
        in_specs=[ANY] * 15 + [VMEM],
        out_specs=(ANY, VMEM),
        scratch_shapes=[
            pltpu.VMEM((D, M), bf16),
            pltpu.VMEM((NY * NZ * GAIN_ROWS, M), bf16),
            pltpu.VMEM((D, 128), f32),
            pltpu.VMEM((ROWS, KV, DEEP), bf16),
            pltpu.VMEM((KV, M), f32),
            pltpu.SemaphoreType.DMA((copies,)),
            pltpu.SemaphoreType.DMA((ROWS,)),
        ],
        compiler_params=pltpu.CompilerParams(vmem_limit_bytes=VMEM_LIMIT),
        cost_estimate=pl.CostEstimate(
            flops=2 * D * M * KV, bytes_accessed=20 * 2**20, transcendentals=0
        ),
        name="norm_kv",
    )(*first, *second, weights, k_gain)


def query_up_kernel(normed, w_one, w_two, q_gain, q_out, hidden_out, sums):
    step = pl.program_id(0)

    @pl.when(step == 0)
    def _():
        sums[...] = jnp.zeros_like(sums)

    rows = normed[...]
    sums[:256, :] += jnp.dot(w_one[0, 0], rows, preferred_element_type=f32)
    sums[256:, :] += jnp.dot(w_two[0, 0], rows, preferred_element_type=f32)

    @pl.when(step == ROWS - 1)
    def _():
        q_out[...] = head_norm(sums[:HD, :], q_gain[...]).astype(bf16)
        hidden_out[...] = jax.nn.gelu(sums[HD:, :]).astype(bf16)


def query_up(normed, weights, q_gain):
    weights = weights.reshape(ROWS, 3, 256, DEEP)
    return pl.pallas_call(
        query_up_kernel,
        grid=(ROWS,),
        out_shape=(jax.ShapeDtypeStruct((HD, M), bf16), jax.ShapeDtypeStruct((FFL, M), bf16)),
        in_specs=[
            pl.BlockSpec((DEEP, M), lambda r: (r, 0)),
            pl.BlockSpec((1, 1, 256, DEEP), lambda r: (r, 1, 0, 0)),
            pl.BlockSpec((1, 1, 256, DEEP), lambda r: (r, 2, 0, 0)),
            pl.BlockSpec((HD, M), lambda r: (0, 0)),
        ],
        out_specs=(
            pl.BlockSpec((HD, M), lambda r: (0, 0)),
            pl.BlockSpec((FFL, M), lambda r: (0, 0)),
        ),
        scratch_shapes=[pltpu.VMEM((QU, M), f32)],
        compiler_params=pltpu.CompilerParams(vmem_limit_bytes=VMEM_LIMIT),
        cost_estimate=pl.CostEstimate(
            flops=2 * D * M * QU, bytes_accessed=14 * 2**20, transcendentals=FFL * M
        ),
        name="query_up",
    )(normed, weights, weights, q_gain)


def attend_kernel(*refs):
    pieces, query, out, scores = refs[:ROWS], refs[ROWS], refs[ROWS + 1], refs[ROWS + 2]
    largest = jnp.full((1, M), -jnp.inf, f32)
    for place, piece in enumerate(pieces):
        part = lax.dot_general(
            piece[:HD, :], query[...], (((0,), (0,)), ((), ())), preferred_element_type=f32
        ) * (1.0 / math.sqrt(HD))
        scores[place * M : (place + 1) * M, :] = part
        largest = jnp.maximum(largest, jnp.max(part, axis=0, keepdims=True))
    total = jnp.zeros((1, M), f32)
    for place in range(ROWS):
        part = jnp.exp(scores[place * M : (place + 1) * M, :] - largest)
        scores[place * M : (place + 1) * M, :] = part
        total = total + jnp.sum(part, axis=0, keepdims=True)
    share = 1.0 / total
    sums = jnp.zeros((HD, M), f32)
    for place, piece in enumerate(pieces):
        probs = (scores[place * M : (place + 1) * M, :] * share).astype(bf16)
        sums = sums + jnp.dot(piece[HD:, :], probs, preferred_element_type=f32)
    out[...] = sums.astype(bf16)


def attend(pieces, query):
    return pl.pallas_call(
        attend_kernel,
        out_shape=jax.ShapeDtypeStruct((HD, M), bf16),
        in_specs=[VMEM] * (ROWS + 1),
        out_specs=VMEM,
        scratch_shapes=[pltpu.VMEM((ROWS * M, M), f32)],
        compiler_params=pltpu.CompilerParams(vmem_limit_bytes=VMEM_LIMIT),
        cost_estimate=pl.CostEstimate(
            flops=20 * ROWS * M * M * HD, bytes_accessed=3 * 2**20, transcendentals=ROWS * M * M
        ),
        name="attend",
    )(*pieces, query)


def gather_copies(refs, weights, held, w_held, rows, columns):
    y, z = position()
    copies = []
    for ref, place, begin, count in piece_rows(refs, rows):
        z_from = back_from(z, Z_OFF[place], NZ)
        row = pl.multiple_of(z_from * rows + begin, 16)
        copies.append((ref, held.at[pl.ds(row, count)]))
    for step in range(NY):
        x_from = lax.rem(2 * y + step, NX)
        for core in range(2):
            copies.append((weights.at[2 * x_from + core, :, columns], w_held.at[2 * step + core]))
    return copies


def hidden_part_kernel(*refs):
    pieces, weights, out, held, w_held, sems = refs[:9], *refs[9:]
    started = start_all(
        gather_copies(pieces, weights, held, w_held, FFL, pl.ds(0, DOWN_K)), sems
    )
    for copy in started:
        copy.wait()
    for step in range(NY):
        out[step] = jnp.dot(
            w_held[2 * step], held[:DOWN_K, :], preferred_element_type=f32
        ) + jnp.dot(w_held[2 * step + 1], held[DOWN_K:, :], preferred_element_type=f32)


def hidden_part(pieces, weights):
    return pl.pallas_call(
        hidden_part_kernel,
        out_shape=jax.ShapeDtypeStruct((NY, BLOCK, M), f32),
        in_specs=[ANY] * 10,
        out_specs=VMEM,
        scratch_shapes=[
            pltpu.VMEM((2 * DOWN_K, M), bf16),
            pltpu.VMEM((ROWS, BLOCK, DOWN_K), bf16),
            pltpu.SemaphoreType.DMA((9 + ROWS,)),
        ],
        compiler_params=pltpu.CompilerParams(vmem_limit_bytes=VMEM_LIMIT),
        cost_estimate=pl.CostEstimate(
            flops=2 * NY * BLOCK * M * 2 * DOWN_K, bytes_accessed=10 * 2**20, transcendentals=0
        ),
        name="hidden_part",
    )(*pieces, weights)


def attended_part_kernel(*refs):
    pieces, weights, part = refs[:8], refs[8], refs[9]
    outs, (held, w_held, sems) = refs[10:14], refs[14:]
    started = start_all(
        gather_copies(pieces, weights, held, w_held, HD, pl.ds(DOWN_K, OUT_K)), sems
    )
    for copy in started:
        copy.wait()
    for step in range(NY):
        total = jnp.dot(w_held[2 * step], held[:OUT_K, :], preferred_element_type=f32)
        total = total + jnp.dot(
            w_held[2 * step + 1], held[OUT_K:, :], preferred_element_type=f32
        )
        outs[step][...] = part[step] + total


def attended_part(pieces, weights, part):
    return pl.pallas_call(
        attended_part_kernel,
        out_shape=(jax.ShapeDtypeStruct((BLOCK, M), f32),) * NY,
        in_specs=[ANY] * 9 + [VMEM],
        out_specs=(VMEM,) * NY,
        scratch_shapes=[
            pltpu.VMEM((2 * OUT_K, M), bf16),
            pltpu.VMEM((ROWS, BLOCK, OUT_K), bf16),
            pltpu.SemaphoreType.DMA((8 + ROWS,)),
        ],
        compiler_params=pltpu.CompilerParams(vmem_limit_bytes=VMEM_LIMIT),
        cost_estimate=pl.CostEstimate(
            flops=2 * NY * BLOCK * M * 2 * OUT_K, bytes_accessed=7 * 2**20, transcendentals=0
        ),
        name="attended_part",
    )(*pieces, weights, part)


def on_device(
    tokens,
    ln_gain,
    q_weight,
    k_weight,
    v_weight,
    up_weight,
    out_weight,
    down_weight,
    q_gain,
    k_gain,
):
    columns = tokens.T
    in_weights = jnp.concatenate([k_weight.T, v_weight.T, q_weight.T, up_weight.T], axis=0)
    in_weights = lax.all_gather(in_weights, "row", axis=0, tiled=False)

    gain_tile = jnp.broadcast_to(jnp.pad(ln_gain, (0, M - BLOCK))[None, :], (GAIN_ROWS, M))
    part1 = jnp.concatenate([columns[:FIRST], gain_tile], axis=0)
    part2 = columns[FIRST:]
    part1 = jnp.concatenate(
        [part1, along_col(part1, 1, 0), along_col(part1, -1, 0), along_col(part1, 2, 0)], axis=0
    )
    first = z_ring(part1, NY * PART1 // 2)
    part2 = jnp.concatenate(z_ring(part2), axis=0)
    forth, back = along_col(part2, 1, 0), along_col(part2, -1, 0)
    half = NZ * PART2 // 2
    second = [part2, forth, back, along_col(forth[:half], 1, 0), along_col(back[half:], -1, 0)]

    out_weights = jnp.concatenate([down_weight.T, out_weight.T], axis=1)
    pairs = [
        (
            (x * 2 + c) * NY * NZ + y * NZ + z,
            (((x + y) % NX) * 2 + c) * NY * NZ + x * NZ + z,
        )
        for x in range(NX)
        for c in range(2)
        for y in range(NY)
        for z in range(NZ)
    ]
    out_weights = lax.ppermute(out_weights, ("row", "col"), pairs)
    out_weights = lax.all_gather(out_weights, "row", axis=0, tiled=False)

    wide = lambda gain: jnp.broadcast_to(gain.reshape(HD, 1), (HD, M))
    normed, own_kv = norm_kv(first, second, in_weights, wide(k_gain))
    kv = [own_kv, along_row(own_kv, 1, 0), along_row(own_kv, -1, 0), along_row(own_kv, 2, 0)]
    kv += [along_row(piece, 0, 1) for piece in kv]
    query, hidden = query_up(normed, in_weights, wide(q_gain))
    part = hidden_part(z_ring(hidden, FFL // 2), out_weights)
    attended = attend(kv, query)
    parts = attended_part(z_ring(attended), out_weights, part)
    summed = columns.astype(f32) + parts[0]
    for step in range(1, NY):
        summed = summed + along_col(parts[step], step, 0)
    return summed.astype(bf16).T


def solution(mesh):
    return jax.shard_map(
        on_device,
        mesh=mesh,
        in_specs=(
            P("row", "col"),
            P("col"),
            P("row", "col"),
            P("row", "col"),
            P("row", "col"),
            P("row", "col"),
            P("row", "col"),
            P("row", "col"),
            P("col", None),
            P("col", None),
        ),
        out_specs=P("row", "col"),
        check_vma=False,
    )
```

```python
import math

import jax
import jax.numpy as jnp
from jax import lax
from jax.experimental import pallas as pl
from jax.experimental.pallas import tpu as pltpu
from jax.sharding import PartitionSpec as P

D = 6144
HD = 128
NX, NY, NZ = 4, 4, 8
ROWS = 2 * NX
M = 512
BLOCK = D // (NY * NZ)
FIRST = 80
GAIN_ROWS = 16
PART1 = FIRST + GAIN_ROWS
PART2 = BLOCK - FIRST
DEEP = D // ROWS
FFL = 384
KV = 2 * HD
QU = HD + FFL
OUT_K = 512
DOWN_K = 1536
Y_OFF = (0, 1, 3, 2)
Z_OFF = (0, 1, 7, 2, 6, 3, 5, 4)
epsilon = 1e-06
f32, bf16 = jnp.float32, jnp.bfloat16
VMEM_LIMIT = 56 * 1024 * 1024
ANY = pl.BlockSpec(memory_space=pl.ANY)
VMEM = pl.BlockSpec(memory_space=pltpu.VMEM)


def along_col(value, dy, dz):
    pairs = [
        (y * NZ + z, ((y + dy) % NY) * NZ + (z + dz) % NZ) for y in range(NY) for z in range(NZ)
    ]
    return lax.ppermute(value, "col", pairs)


def along_row(value, dx, dc):
    pairs = [
        (x * 2 + c, ((x + dx) % NX) * 2 + (c + dc) % 2) for x in range(NX) for c in range(2)
    ]
    return lax.ppermute(value, "row", pairs)


def z_ring(block, half=None):
    forth = back = block
    blocks = [block]
    for _ in range(3):
        forth, back = along_col(forth, 0, 1), along_col(back, 0, -1)
        blocks += [forth, back]
    if half is None:
        return blocks + [along_col(forth, 0, 1)]
    return blocks + [along_col(forth[:half], 0, 1), along_col(back[half:], 0, -1)]


def position():
    col = lax.axis_index("col")
    return lax.div(col, NZ), lax.rem(col, NZ)


def back_from(index, offset, size):
    return lax.rem(index + (size - offset), size)


def start_all(copies, sems):
    started = []
    for number, (source, target) in enumerate(copies):
        copy = pltpu.make_async_copy(source, target, sems.at[number])
        copy.start()
        started.append(copy)
    return started


def head_norm(values, gain):
    average = jnp.mean(values, axis=0, keepdims=True)
    variance = jnp.mean(values * values, axis=0, keepdims=True) - average * average
    return (values - average) * lax.rsqrt(variance + epsilon) * gain


def piece_rows(refs, rows):
    spans = [(ref, place, 0, rows) for place, ref in enumerate(refs[:7])]
    if len(refs) == 8:
        return spans + [(refs[7], 7, 0, rows)]
    half = refs[7].shape[0]
    return spans + [(refs[7], 7, 0, half), (refs[8], 7, half, rows - half)]


def turn_kernel(k_weight, v_weight, q_weight, up_weight, out):
    begin = 0
    for weight in (k_weight, v_weight, q_weight, up_weight):
        for step in range(weight.shape[1] // HD):
            columns = weight[:, step * HD : (step + 1) * HD]
            out[begin : begin + HD, :] = columns.T
            begin += HD


def turn(*weights):
    return pl.pallas_call(
        turn_kernel,
        out_shape=jax.ShapeDtypeStruct((KV + QU, DEEP), bf16),
        in_specs=[VMEM] * 4,
        out_specs=VMEM,
        compiler_params=pltpu.CompilerParams(vmem_limit_bytes=VMEM_LIMIT),
        cost_estimate=pl.CostEstimate(flops=0, bytes_accessed=3 * 2**20, transcendentals=0),
        name="turn",
    )(*weights)


def project_all_kernel(*refs):
    first, second = refs[:9], refs[9:14]
    weights, k_gain, q_gain, kv_out, q_out, hidden_out = refs[14:20]
    held, gains, gain_wide, w_held, sums, sems = refs[20:]
    y, z = position()
    copies = []
    for ref, place, begin, rows in piece_rows(first, NY * PART1):
        z_from = back_from(z, Z_OFF[place], NZ)
        for sub in range(rows // PART1):
            y_from = back_from(y, Y_OFF[begin // PART1 + sub], NY)
            block = y_from * NZ + z_from
            row = pl.multiple_of(block * BLOCK, 16)
            copies.append((ref.at[pl.ds(sub * PART1, FIRST)], held.at[pl.ds(row, FIRST)]))
            row = pl.multiple_of(block * GAIN_ROWS, 16)
            copies.append(
                (ref.at[pl.ds(sub * PART1 + FIRST, GAIN_ROWS)], gains.at[pl.ds(row, GAIN_ROWS)])
            )
    spans = [(second[0], 0, 0, 8), (second[1], 1, 0, 8), (second[2], 2, 0, 8)]
    spans += [(second[3], 3, 0, 4), (second[4], 3, 4, 4)]
    for ref, place, begin, count in spans:
        y_from = back_from(y, Y_OFF[place], NY)
        for sub in range(count):
            z_from = back_from(z, Z_OFF[begin + sub], NZ)
            row = pl.multiple_of((y_from * NZ + z_from) * BLOCK + FIRST, 16)
            copies.append((ref.at[pl.ds(sub * PART2, PART2)], held.at[pl.ds(row, PART2)]))
    for part in range(ROWS):
        copies.append((weights.at[part], w_held.at[part]))
    started = start_all(copies, sems)
    for copy in started[:-ROWS]:
        copy.wait()

    gain_rows = jnp.max(gains[:, :256].astype(f32).reshape(NY * NZ, GAIN_ROWS, 256), axis=1)
    gain_columns = gain_rows.T
    for block in range(NY * NZ):
        gain_wide[block * BLOCK : (block + 1) * BLOCK, :] = jnp.broadcast_to(
            gain_columns[:BLOCK, block : block + 1], (BLOCK, 128)
        )

    chunk = 96

    def add(step, totals):
        rows = held[pl.ds(pl.multiple_of(step * chunk, chunk), chunk), :].astype(f32)
        rows = rows.reshape(chunk // 8, 8, M)
        return totals[0] + jnp.sum(rows, axis=0), totals[1] + jnp.sum(rows * rows, axis=0)

    zero = jnp.zeros((8, M), f32)
    totals = lax.fori_loop(0, D // chunk, add, (zero, zero))
    average = jnp.sum(totals[0], axis=0, keepdims=True) / D
    variance = jnp.sum(totals[1], axis=0, keepdims=True) / D - average * average
    scale = lax.rsqrt(variance + epsilon)
    for copy in started[-ROWS:]:
        copy.wait()
    sums[...] = jnp.zeros_like(sums)

    def project(part, _):
        def norm(step, _):
            where = pl.ds(pl.multiple_of(part * DEEP + step * chunk, chunk), chunk)
            gain = jnp.concatenate([gain_wide[where, :]] * 4, axis=1)
            rows = held[where, :].astype(f32)
            held[where, :] = ((rows - average) * scale * gain).astype(bf16)
            return 0

        lax.fori_loop(0, DEEP // chunk, norm, 0)
        where = pl.ds(pl.multiple_of(part * DEEP, DEEP), DEEP)
        sums[...] += jnp.dot(w_held[part], held[where, :], preferred_element_type=f32)
        return 0

    lax.fori_loop(0, ROWS, project, 0)
    kv_out[:HD, :] = head_norm(sums[:HD, :], k_gain[...]).astype(bf16)
    kv_out[HD:, :] = sums[HD:KV, :].astype(bf16)
    q_out[...] = head_norm(sums[KV : KV + HD, :], q_gain[...]).astype(bf16)
    hidden_out[...] = jax.nn.gelu(sums[KV + HD :, :]).astype(bf16)


def project_all(first, second, weights, k_gain, q_gain):
    copies = 64 + 32 + ROWS
    return pl.pallas_call(
        project_all_kernel,
        out_shape=(
            jax.ShapeDtypeStruct((KV, M), bf16),
            jax.ShapeDtypeStruct((HD, M), bf16),
            jax.ShapeDtypeStruct((FFL, M), bf16),
        ),
        in_specs=[ANY] * 15 + [VMEM] * 2,
        out_specs=(VMEM, VMEM, VMEM),
        scratch_shapes=[
            pltpu.VMEM((D, M), bf16),
            pltpu.VMEM((NY * NZ * GAIN_ROWS, M), bf16),
            pltpu.VMEM((D, 128), f32),
            pltpu.VMEM((ROWS, KV + QU, DEEP), bf16),
            pltpu.VMEM((KV + QU, M), f32),
            pltpu.SemaphoreType.DMA((copies,)),
        ],
        compiler_params=pltpu.CompilerParams(vmem_limit_bytes=VMEM_LIMIT),
        cost_estimate=pl.CostEstimate(
            flops=2 * D * M * (KV + QU), bytes_accessed=18 * 2**20, transcendentals=FFL * M
        ),
        name="project_all",
    )(*first, *second, weights, k_gain, q_gain)


def attend_kernel(*refs):
    pieces, query, out, scores = refs[:ROWS], refs[ROWS], refs[ROWS + 1], refs[ROWS + 2]
    largest = jnp.full((1, M), -jnp.inf, f32)
    for place, piece in enumerate(pieces):
        part = lax.dot_general(
            piece[:HD, :], query[...], (((0,), (0,)), ((), ())), preferred_element_type=f32
        ) * (1.0 / math.sqrt(HD))
        scores[place * M : (place + 1) * M, :] = part
        largest = jnp.maximum(largest, jnp.max(part, axis=0, keepdims=True))
    total = jnp.zeros((1, M), f32)
    for place in range(ROWS):
        part = jnp.exp(scores[place * M : (place + 1) * M, :] - largest)
        scores[place * M : (place + 1) * M, :] = part
        total = total + jnp.sum(part, axis=0, keepdims=True)
    share = 1.0 / total
    sums = jnp.zeros((HD, M), f32)
    for place, piece in enumerate(pieces):
        probs = (scores[place * M : (place + 1) * M, :] * share).astype(bf16)
        sums = sums + jnp.dot(piece[HD:, :], probs, preferred_element_type=f32)
    out[...] = sums.astype(bf16)


def attend(pieces, query):
    return pl.pallas_call(
        attend_kernel,
        out_shape=jax.ShapeDtypeStruct((HD, M), bf16),
        in_specs=[VMEM] * (ROWS + 1),
        out_specs=VMEM,
        scratch_shapes=[pltpu.VMEM((ROWS * M, M), f32)],
        compiler_params=pltpu.CompilerParams(vmem_limit_bytes=VMEM_LIMIT),
        cost_estimate=pl.CostEstimate(
            flops=20 * ROWS * M * M * HD, bytes_accessed=3 * 2**20, transcendentals=ROWS * M * M
        ),
        name="attend",
    )(*pieces, query)


def gather_copies(refs, weights, held, w_held, rows, columns):
    y, z = position()
    copies = []
    for ref, place, begin, count in piece_rows(refs, rows):
        z_from = back_from(z, Z_OFF[place], NZ)
        row = pl.multiple_of(z_from * rows + begin, 16)
        copies.append((ref, held.at[pl.ds(row, count)]))
    for step in range(NY):
        x_from = lax.rem(2 * y + step, NX)
        for core in range(2):
            copies.append((weights.at[2 * x_from + core, :, columns], w_held.at[2 * step + core]))
    return copies


def hidden_part_kernel(*refs):
    pieces, weights, out, held, w_held, sems = refs[:9], *refs[9:]
    started = start_all(
        gather_copies(pieces, weights, held, w_held, FFL, pl.ds(0, DOWN_K)), sems
    )
    for copy in started:
        copy.wait()
    for step in range(NY):
        out[step] = jnp.dot(
            w_held[2 * step], held[:DOWN_K, :], preferred_element_type=f32
        ) + jnp.dot(w_held[2 * step + 1], held[DOWN_K:, :], preferred_element_type=f32)


def hidden_part(pieces, weights):
    return pl.pallas_call(
        hidden_part_kernel,
        out_shape=jax.ShapeDtypeStruct((NY, BLOCK, M), f32),
        in_specs=[ANY] * 10,
        out_specs=VMEM,
        scratch_shapes=[
            pltpu.VMEM((2 * DOWN_K, M), bf16),
            pltpu.VMEM((ROWS, BLOCK, DOWN_K), bf16),
            pltpu.SemaphoreType.DMA((9 + ROWS,)),
        ],
        compiler_params=pltpu.CompilerParams(vmem_limit_bytes=VMEM_LIMIT),
        cost_estimate=pl.CostEstimate(
            flops=2 * NY * BLOCK * M * 2 * DOWN_K, bytes_accessed=10 * 2**20, transcendentals=0
        ),
        name="hidden_part",
    )(*pieces, weights)


def attended_part_kernel(*refs):
    pieces, weights, part = refs[:8], refs[8], refs[9]
    outs, (held, w_held, part_held, sems) = refs[10:14], refs[14:]
    copies = gather_copies(pieces, weights, held, w_held, HD, pl.ds(DOWN_K, OUT_K))
    started = start_all(copies + [(part, part_held)], sems)
    for copy in started:
        copy.wait()
    for step in range(NY):
        total = jnp.dot(w_held[2 * step], held[:OUT_K, :], preferred_element_type=f32)
        total = total + jnp.dot(
            w_held[2 * step + 1], held[OUT_K:, :], preferred_element_type=f32
        )
        outs[step][...] = (part_held[step] + total).astype(outs[step].dtype)


def attended_part(pieces, weights, part):
    shape = (BLOCK, M)
    return pl.pallas_call(
        attended_part_kernel,
        out_shape=(jax.ShapeDtypeStruct(shape, f32),) + (jax.ShapeDtypeStruct(shape, bf16),) * 3,
        in_specs=[ANY] * 10,
        out_specs=(VMEM,) * NY,
        scratch_shapes=[
            pltpu.VMEM((2 * OUT_K, M), bf16),
            pltpu.VMEM((ROWS, BLOCK, OUT_K), bf16),
            pltpu.VMEM((NY, BLOCK, M), f32),
            pltpu.SemaphoreType.DMA((9 + ROWS,)),
        ],
        compiler_params=pltpu.CompilerParams(vmem_limit_bytes=VMEM_LIMIT),
        cost_estimate=pl.CostEstimate(
            flops=2 * NY * BLOCK * M * 2 * OUT_K, bytes_accessed=7 * 2**20, transcendentals=0
        ),
        name="attended_part",
    )(*pieces, weights, part)


def after(value, *others):
    return lax.optimization_barrier((value, *others))[0]


def on_device(
    tokens,
    ln_gain,
    q_weight,
    k_weight,
    v_weight,
    up_weight,
    out_weight,
    down_weight,
    q_gain,
    k_gain,
):
    columns = tokens.T
    in_weights = turn(k_weight, v_weight, q_weight, up_weight)
    in_weights = lax.all_gather(in_weights, "row", axis=0, tiled=False)

    gain_tile = jnp.broadcast_to(jnp.pad(ln_gain, (0, M - BLOCK))[None, :], (GAIN_ROWS, M))
    part1 = jnp.concatenate([columns[:FIRST], gain_tile], axis=0)
    part1 = jnp.concatenate(
        [part1, along_col(part1, 1, 0), along_col(part1, -1, 0), along_col(part1, 2, 0)], axis=0
    )
    first = z_ring(part1, NY * PART1 // 2)
    part2 = jnp.concatenate(z_ring(columns[FIRST:]), axis=0)
    part2 = after(part2, first[1], first[2])
    forth, back = along_col(part2, 1, 0), along_col(part2, -1, 0)
    half = NZ * PART2 // 2
    top, bottom = after(forth[:half], first[5], first[6]), after(back[half:], first[5], first[6])
    second = [part2, forth, back, along_col(top, 1, 0), along_col(bottom, -1, 0)]

    out_weights = jnp.concatenate([down_weight.T, out_weight.T], axis=1)
    out_weights = after(out_weights, part2)
    pairs = [
        (
            (x * 2 + c) * NY * NZ + y * NZ + z,
            (((x + y) % NX) * 2 + c) * NY * NZ + x * NZ + z,
        )
        for x in range(NX)
        for c in range(2)
        for y in range(NY)
        for z in range(NZ)
    ]
    out_weights = lax.ppermute(out_weights, ("row", "col"), pairs)

    wide = lambda gain: jnp.broadcast_to(gain.reshape(HD, 1), (HD, M))
    out_weights = after(out_weights, first[5], first[6], forth, back)
    k_wide = after(wide(k_gain), out_weights)
    out_weights = lax.all_gather(out_weights, "row", axis=0, tiled=False)
    own_kv, query, hidden = project_all(first, second, in_weights, k_wide, wide(q_gain))
    kv = [own_kv, along_row(own_kv, 1, 0), along_row(own_kv, -1, 0), along_row(own_kv, 2, 0)]
    kv += [along_row(piece, 0, 1) for piece in kv]
    part = hidden_part(z_ring(hidden, FFL // 2), out_weights)
    attended = attend(kv, query)
    parts = attended_part(z_ring(attended), out_weights, part)
    summed = columns.astype(f32) + parts[0]
    for step in range(1, NY):
        summed = summed + along_col(parts[step], step, 0).astype(f32)
    return summed.astype(bf16).T


def solution(mesh):
    return jax.shard_map(
        on_device,
        mesh=mesh,
        in_specs=(
            P("row", "col"),
            P("col"),
            P("row", "col"),
            P("row", "col"),
            P("row", "col"),
            P("row", "col"),
            P("row", "col"),
            P("row", "col"),
            P("col", None),
            P("col", None),
        ),
        out_specs=P("row", "col"),
        check_vma=False,
    )
```

```python
import math

import jax
import jax.numpy as jnp
from jax import lax
from jax.experimental import pallas as pl
from jax.experimental.pallas import tpu as pltpu
from jax.sharding import PartitionSpec as P

D = 6144
HD = 128
NX, NY, NZ = 4, 4, 8
ROWS = 2 * NX
M = 512
BLOCK = D // (NY * NZ)
FIRST = 96
GAIN_ROWS = 16
PART1 = FIRST + GAIN_ROWS
PART2 = BLOCK - FIRST
DEEP = D // ROWS
FFL = 384
KV = 2 * HD
QU = HD + FFL
OUT_K = 512
DOWN_K = 1536
OUT_ROWS = DOWN_K + OUT_K
Y_OFF = (0, 1, 3, 2)
Z_OFF = (0, 1, 7, 2, 6, 3, 5, 4)
epsilon = 1e-06
f32, bf16 = jnp.float32, jnp.bfloat16
VMEM_LIMIT = 56 * 1024 * 1024
ANY = pl.BlockSpec(memory_space=pl.ANY)
VMEM = pl.BlockSpec(memory_space=pltpu.VMEM)


def along_col(value, dy, dz):
    pairs = [
        (y * NZ + z, ((y + dy) % NY) * NZ + (z + dz) % NZ) for y in range(NY) for z in range(NZ)
    ]
    return lax.ppermute(value, "col", pairs)


def along_row(value, dx, dc):
    pairs = [
        (x * 2 + c, ((x + dx) % NX) * 2 + (c + dc) % 2) for x in range(NX) for c in range(2)
    ]
    return lax.ppermute(value, "row", pairs)


def z_ring(block, half=None):
    forth = back = block
    blocks = [block]
    for _ in range(3):
        forth, back = along_col(forth, 0, 1), along_col(back, 0, -1)
        blocks += [forth, back]
    if half is None:
        return blocks + [along_col(forth, 0, 1)]
    return blocks + [along_col(forth[:half], 0, 1), along_col(back[half:], 0, -1)]


def position():
    col = lax.axis_index("col")
    return lax.div(col, NZ), lax.rem(col, NZ)


def back_from(index, offset, size):
    return lax.rem(index + (size - offset), size)


def start_all(copies, sems):
    started = []
    for number, (source, target) in enumerate(copies):
        copy = pltpu.make_async_copy(source, target, sems.at[number])
        copy.start()
        started.append(copy)
    return started


def head_norm(values, gain):
    average = jnp.mean(values, axis=0, keepdims=True)
    variance = jnp.mean(values * values, axis=0, keepdims=True) - average * average
    return (values - average) * lax.rsqrt(variance + epsilon) * gain


def piece_rows(refs, rows):
    spans = [(ref, place, 0, rows) for place, ref in enumerate(refs[:7])]
    if len(refs) == 8:
        return spans + [(refs[7], 7, 0, rows)]
    half = refs[7].shape[0]
    return spans + [(refs[7], 7, 0, half), (refs[8], 7, half, rows - half)]


def turn_kernel(k_weight, v_weight, q_weight, up_weight, out):
    begin = 0
    for weight in (k_weight, v_weight, q_weight, up_weight):
        for step in range(weight.shape[1] // HD):
            columns = weight[:, step * HD : (step + 1) * HD]
            out[begin : begin + HD, :] = columns.T
            begin += HD


def turn(*weights):
    return pl.pallas_call(
        turn_kernel,
        out_shape=jax.ShapeDtypeStruct((KV + QU, DEEP), bf16),
        in_specs=[VMEM] * 4,
        out_specs=VMEM,
        compiler_params=pltpu.CompilerParams(vmem_limit_bytes=VMEM_LIMIT),
        cost_estimate=pl.CostEstimate(flops=0, bytes_accessed=3 * 2**20, transcendentals=0),
        name="turn",
    )(*weights)


def add_rows(totals, rows):
    rows = rows.astype(f32).reshape(rows.shape[0] // 8, 8, M)
    return totals[0] + jnp.sum(rows, axis=0), totals[1] + jnp.sum(rows * rows, axis=0)


def early_sums_kernel(*refs):
    zero = jnp.zeros((8, M), f32)
    totals = zero, zero
    for piece in refs[:7]:
        for sub in range(NY):
            totals = add_rows(totals, piece[sub * PART1 : sub * PART1 + FIRST, :])
    for piece in refs[7:10]:
        for sub in range(NZ):
            totals = add_rows(totals, piece[sub * PART2 : (sub + 1) * PART2, :])
    refs[10][...], refs[11][...] = totals


def early_sums(pieces):
    return pl.pallas_call(
        early_sums_kernel,
        out_shape=(jax.ShapeDtypeStruct((8, M), f32),) * 2,
        in_specs=[VMEM] * 10,
        out_specs=(VMEM, VMEM),
        compiler_params=pltpu.CompilerParams(vmem_limit_bytes=VMEM_LIMIT),
        cost_estimate=pl.CostEstimate(
            flops=20 * D * M, bytes_accessed=6 * 2**20, transcendentals=0
        ),
        name="early_sums",
    )(*pieces)


def project_all_kernel(*refs):
    first, second = refs[:9], refs[9:14]
    sum_early, square_early, weights, k_gain, q_gain = refs[14:19]
    kv_out, q_out, hidden_out, held, normed, gains, gain_wide, w_held, sums, sems = refs[19:]
    y, z = position()
    copies = []
    for ref, place, begin, rows in piece_rows(first, NY * PART1):
        z_from = back_from(z, Z_OFF[place], NZ)
        for sub in range(rows // PART1):
            y_from = back_from(y, Y_OFF[begin // PART1 + sub], NY)
            block = y_from * NZ + z_from
            row = pl.multiple_of(block * BLOCK, 16)
            copies.append((ref.at[pl.ds(sub * PART1, FIRST)], held.at[pl.ds(row, FIRST)]))
            row = pl.multiple_of(block * GAIN_ROWS, 16)
            copies.append(
                (ref.at[pl.ds(sub * PART1 + FIRST, GAIN_ROWS)], gains.at[pl.ds(row, GAIN_ROWS)])
            )
    spans = [(second[0], 0, 0, 8), (second[1], 1, 0, 8), (second[2], 2, 0, 8)]
    spans += [(second[3], 3, 0, 4), (second[4], 3, 4, 4)]
    for ref, place, begin, count in spans:
        y_from = back_from(y, Y_OFF[place], NY)
        for sub in range(count):
            z_from = back_from(z, Z_OFF[begin + sub], NZ)
            row = pl.multiple_of((y_from * NZ + z_from) * BLOCK + FIRST, 16)
            copies.append((ref.at[pl.ds(sub * PART2, PART2)], held.at[pl.ds(row, PART2)]))
    for part in range(ROWS):
        copies.append((weights.at[part], w_held.at[part]))
    started = start_all(copies, sems)
    for copy in started[:-ROWS]:
        copy.wait()

    gain_rows = jnp.max(gains[:, :256].astype(f32).reshape(NY * NZ, GAIN_ROWS, 256), axis=1)
    gain_columns = gain_rows.T
    for block in range(NY * NZ):
        gain_wide[block * BLOCK : (block + 1) * BLOCK, :] = jnp.broadcast_to(
            gain_columns[:BLOCK, block : block + 1], (BLOCK, 128)
        )

    totals = sum_early[...], square_early[...]
    z_far, y_far = back_from(z, 4, NZ), back_from(y, 2, NY)
    late = [(y_from * NZ + z_far) * BLOCK for y_from in range(NY)]
    for row in late:
        totals = add_rows(totals, held[pl.ds(pl.multiple_of(row, 16), FIRST), :])
    late = [(y_far * NZ + z_from) * BLOCK + FIRST for z_from in range(NZ)]
    for row in late:
        totals = add_rows(totals, held[pl.ds(pl.multiple_of(row, 16), PART2), :])
    average = jnp.sum(totals[0], axis=0, keepdims=True) / D
    variance = jnp.sum(totals[1], axis=0, keepdims=True) / D - average * average
    scale = lax.rsqrt(variance + epsilon)
    for copy in started[-ROWS:]:
        copy.wait()

    chunk = 96
    for part in range(ROWS):
        for begin in range(part * DEEP, (part + 1) * DEEP, chunk):
            where = slice(begin, begin + chunk)
            gain = jnp.concatenate([gain_wide[where, :]] * 4, axis=1)
            rows = held[where, :].astype(f32)
            normed[where, :] = ((rows - average) * scale * gain).astype(bf16)
        product = jnp.dot(
            w_held[part], normed[part * DEEP : (part + 1) * DEEP, :], preferred_element_type=f32
        )
        if part == 0:
            sums[...] = product
        else:
            sums[...] += product
    kv_out[:HD, :] = head_norm(sums[:HD, :], k_gain[...]).astype(bf16)
    kv_out[HD:, :] = sums[HD:KV, :].astype(bf16)
    q_out[...] = head_norm(sums[KV : KV + HD, :], q_gain[...]).astype(bf16)
    hidden_out[...] = jax.nn.gelu(sums[KV + HD :, :]).astype(bf16)


def project_all(first, second, early, weights, k_gain, q_gain):
    copies = 64 + 32 + ROWS
    return pl.pallas_call(
        project_all_kernel,
        out_shape=(
            jax.ShapeDtypeStruct((KV, M), bf16),
            jax.ShapeDtypeStruct((HD, M), bf16),
            jax.ShapeDtypeStruct((FFL, M), bf16),
        ),
        in_specs=[ANY] * 14 + [VMEM] * 2 + [ANY] + [VMEM] * 2,
        out_specs=(VMEM, VMEM, VMEM),
        scratch_shapes=[
            pltpu.VMEM((D, M), bf16),
            pltpu.VMEM((D, M), bf16),
            pltpu.VMEM((NY * NZ * GAIN_ROWS, M), bf16),
            pltpu.VMEM((D, 128), f32),
            pltpu.VMEM((ROWS, KV + QU, DEEP), bf16),
            pltpu.VMEM((KV + QU, M), f32),
            pltpu.SemaphoreType.DMA((copies,)),
        ],
        compiler_params=pltpu.CompilerParams(vmem_limit_bytes=VMEM_LIMIT),
        cost_estimate=pl.CostEstimate(
            flops=2 * D * M * (KV + QU), bytes_accessed=18 * 2**20, transcendentals=FFL * M
        ),
        name="project_all",
    )(*first, *second, *early, weights, k_gain, q_gain)


def attend_kernel(*refs):
    pieces, query, out, scores = refs[:ROWS], refs[ROWS], refs[ROWS + 1], refs[ROWS + 2]
    largest = jnp.full((1, M), -jnp.inf, f32)
    for place, piece in enumerate(pieces):
        part = lax.dot_general(
            piece[:HD, :], query[...], (((0,), (0,)), ((), ())), preferred_element_type=f32
        ) * (1.0 / math.sqrt(HD))
        scores[place * M : (place + 1) * M, :] = part
        largest = jnp.maximum(largest, jnp.max(part, axis=0, keepdims=True))
    total = jnp.zeros((1, M), f32)
    for place in range(ROWS):
        part = jnp.exp(scores[place * M : (place + 1) * M, :] - largest)
        scores[place * M : (place + 1) * M, :] = part
        total = total + jnp.sum(part, axis=0, keepdims=True)
    share = 1.0 / total
    sums = jnp.zeros((HD, M), f32)
    for place, piece in enumerate(pieces):
        probs = (scores[place * M : (place + 1) * M, :] * share).astype(bf16)
        sums = sums + jnp.dot(piece[HD:, :], probs, preferred_element_type=f32)
    out[...] = sums.astype(bf16)


def attend(pieces, query):
    return pl.pallas_call(
        attend_kernel,
        out_shape=jax.ShapeDtypeStruct((HD, M), bf16),
        in_specs=[VMEM] * (ROWS + 1),
        out_specs=VMEM,
        scratch_shapes=[pltpu.VMEM((ROWS * M, M), f32)],
        compiler_params=pltpu.CompilerParams(vmem_limit_bytes=VMEM_LIMIT),
        cost_estimate=pl.CostEstimate(
            flops=20 * ROWS * M * M * HD, bytes_accessed=3 * 2**20, transcendentals=ROWS * M * M
        ),
        name="attend",
    )(*pieces, query)


def out_part_kernel(*refs):
    hidden, attended, weights, outs = refs[:9], refs[9:17], refs[17], refs[18:22]
    held, w_held, sems = refs[22:]
    y, z = position()
    copies = []
    for pieces, rows, first_row in ((hidden, FFL, 0), (attended, HD, DOWN_K)):
        for ref, place, begin, count in piece_rows(pieces, rows):
            z_from = back_from(z, Z_OFF[place], NZ)
            row = lax.div(z_from, 4) * OUT_ROWS + lax.rem(z_from, 4) * rows + (first_row + begin)
            copies.append((ref, held.at[pl.ds(pl.multiple_of(row, 16), count)]))
    for step in range(NY):
        x_from = lax.rem(2 * y + step, NX)
        for core in range(2):
            copies.append((weights.at[2 * x_from + core], w_held.at[2 * step + core]))
    started = start_all(copies, sems)
    for copy in started[:17]:
        copy.wait()
    for step in range(NY):
        started[17 + 2 * step].wait()
        started[18 + 2 * step].wait()
        total = jnp.dot(w_held[2 * step], held[:OUT_ROWS, :], preferred_element_type=f32)
        total = total + jnp.dot(
            w_held[2 * step + 1], held[OUT_ROWS:, :], preferred_element_type=f32
        )
        outs[step][...] = total.astype(outs[step].dtype)


def out_part(hidden, attended, weights):
    shape = (BLOCK, M)
    return pl.pallas_call(
        out_part_kernel,
        out_shape=(jax.ShapeDtypeStruct(shape, f32),) + (jax.ShapeDtypeStruct(shape, bf16),) * 3,
        in_specs=[ANY] * 18,
        out_specs=(VMEM,) * NY,
        scratch_shapes=[
            pltpu.VMEM((2 * OUT_ROWS, M), bf16),
            pltpu.VMEM((ROWS, BLOCK, OUT_ROWS), bf16),
            pltpu.SemaphoreType.DMA((17 + ROWS,)),
        ],
        compiler_params=pltpu.CompilerParams(vmem_limit_bytes=VMEM_LIMIT),
        cost_estimate=pl.CostEstimate(
            flops=4 * NY * BLOCK * M * OUT_ROWS, bytes_accessed=12 * 2**20, transcendentals=0
        ),
        name="out_part",
    )(*hidden, *attended, weights)


def after(value, *others):
    return lax.optimization_barrier((value, *others))[0]


def on_device(
    tokens,
    ln_gain,
    q_weight,
    k_weight,
    v_weight,
    up_weight,
    out_weight,
    down_weight,
    q_gain,
    k_gain,
):
    columns = tokens.T
    in_weights = turn(k_weight, v_weight, q_weight, up_weight)
    in_weights = lax.all_gather(in_weights, "row", axis=0, tiled=False)

    gain_tile = jnp.broadcast_to(jnp.pad(ln_gain, (0, M - BLOCK))[None, :], (GAIN_ROWS, M))
    part1 = jnp.concatenate([columns[:FIRST], gain_tile], axis=0)
    part1 = jnp.concatenate(
        [part1, along_col(part1, 1, 0), along_col(part1, -1, 0), along_col(part1, 2, 0)], axis=0
    )
    first = z_ring(part1, NY * PART1 // 2)
    part2 = jnp.concatenate(z_ring(columns[FIRST:]), axis=0)
    part2 = after(part2, first[3], first[4])
    forth, back = along_col(part2, 1, 0), along_col(part2, -1, 0)
    half = NZ * PART2 // 2
    top, bottom = after(forth[:half], first[5], first[6]), after(back[half:], first[5], first[6])
    second = [part2, forth, back, along_col(top, 1, 0), along_col(bottom, -1, 0)]

    early = early_sums(first[:7] + second[:3])
    out_weights = jnp.concatenate([down_weight.T, out_weight.T], axis=1)
    out_weights = after(out_weights, part2)
    pairs = [
        (
            (x * 2 + c) * NY * NZ + y * NZ + z,
            (((x + y) % NX) * 2 + c) * NY * NZ + x * NZ + z,
        )
        for x in range(NX)
        for c in range(2)
        for y in range(NY)
        for z in range(NZ)
    ]
    out_weights = lax.ppermute(out_weights, ("row", "col"), pairs)

    wide = lambda gain: jnp.broadcast_to(gain.reshape(HD, 1), (HD, M))
    out_weights = after(out_weights, *first[7:], *second[3:], *early)
    k_wide = after(wide(k_gain), out_weights)
    out_weights = lax.all_gather(out_weights, "row", axis=0, tiled=False)
    own_kv, query, hidden = project_all(first, second, early, in_weights, k_wide, wide(q_gain))
    kv = [own_kv, along_row(own_kv, 1, 0), along_row(own_kv, -1, 0), along_row(own_kv, 2, 0)]
    kv += [along_row(piece, 0, 1) for piece in kv]
    hidden = z_ring(hidden, FFL // 2)
    attended = attend(kv, query)
    parts = out_part(hidden, z_ring(attended), out_weights)
    summed = columns.astype(f32) + parts[0]
    for step in range(1, NY):
        summed = summed + along_col(parts[step], step, 0).astype(f32)
    return summed.astype(bf16).T


def solution(mesh):
    return jax.shard_map(
        on_device,
        mesh=mesh,
        in_specs=(
            P("row", "col"),
            P("col"),
            P("row", "col"),
            P("row", "col"),
            P("row", "col"),
            P("row", "col"),
            P("row", "col"),
            P("row", "col"),
            P("col", None),
            P("col", None),
        ),
        out_specs=P("row", "col"),
        check_vma=False,
    )
```

```python
import math

import jax
import jax.numpy as jnp
from jax import lax
from jax.experimental import pallas as pl
from jax.experimental.pallas import tpu as pltpu
from jax.sharding import PartitionSpec as P

D = 6144
HD = 128
NX, NY, NZ = 4, 4, 8
ROWS = 2 * NX
M = 512
BLOCK = D // (NY * NZ)
FIRST = 96
GAIN_ROWS = 16
PART1 = FIRST + GAIN_ROWS
PART2 = BLOCK - FIRST
DEEP = D // ROWS
FFL = 384
KV = 2 * HD
QU = HD + FFL
OUT_K = 512
DOWN_K = 1536
OUT_ROWS = DOWN_K + OUT_K
Y_OFF = (0, 1, 3, 2)
Z_OFF = (0, 1, 7, 2, 6, 3, 5, 4)
epsilon = 1e-06
f32, bf16 = jnp.float32, jnp.bfloat16
VMEM_LIMIT = 56 * 1024 * 1024
ANY = pl.BlockSpec(memory_space=pl.ANY)
VMEM = pl.BlockSpec(memory_space=pltpu.VMEM)


def along_col(value, dy, dz):
    pairs = [
        (y * NZ + z, ((y + dy) % NY) * NZ + (z + dz) % NZ) for y in range(NY) for z in range(NZ)
    ]
    return lax.ppermute(value, "col", pairs)


def along_row(value, dx, dc):
    pairs = [
        (x * 2 + c, ((x + dx) % NX) * 2 + (c + dc) % 2) for x in range(NX) for c in range(2)
    ]
    return lax.ppermute(value, "row", pairs)


def z_ring(block, half=None):
    forth = back = block
    blocks = [block]
    for _ in range(3):
        forth, back = along_col(forth, 0, 1), along_col(back, 0, -1)
        blocks += [forth, back]
    if half is None:
        return blocks + [along_col(forth, 0, 1)]
    return blocks + [along_col(forth[:half], 0, 1), along_col(back[half:], 0, -1)]


def z_direct(block):
    return [block] + [along_col(block, 0, offset) for offset in Z_OFF[1:]]


def position():
    col = lax.axis_index("col")
    return lax.div(col, NZ), lax.rem(col, NZ)


def back_from(index, offset, size):
    return lax.rem(index + (size - offset), size)


def start_all(copies, sems):
    started = []
    for number, (source, target) in enumerate(copies):
        copy = pltpu.make_async_copy(source, target, sems.at[number])
        copy.start()
        started.append(copy)
    return started


def head_norm(values, gain):
    average = jnp.mean(values, axis=0, keepdims=True)
    variance = jnp.mean(values * values, axis=0, keepdims=True) - average * average
    return (values - average) * lax.rsqrt(variance + epsilon) * gain


def piece_rows(refs, rows):
    spans = [(ref, place, 0, rows) for place, ref in enumerate(refs[:7])]
    if len(refs) == 8:
        return spans + [(refs[7], 7, 0, rows)]
    half = refs[7].shape[0]
    return spans + [(refs[7], 7, 0, half), (refs[8], 7, half, rows - half)]


def turn_kernel(k_weight, v_weight, q_weight, up_weight, out):
    begin = 0
    for weight in (k_weight, v_weight, q_weight, up_weight):
        for step in range(weight.shape[1] // HD):
            columns = weight[:, step * HD : (step + 1) * HD]
            out[begin : begin + HD, :] = columns.T
            begin += HD


def turn(*weights):
    return pl.pallas_call(
        turn_kernel,
        out_shape=jax.ShapeDtypeStruct((KV + QU, DEEP), bf16),
        in_specs=[VMEM] * 4,
        out_specs=VMEM,
        compiler_params=pltpu.CompilerParams(vmem_limit_bytes=VMEM_LIMIT),
        cost_estimate=pl.CostEstimate(flops=0, bytes_accessed=3 * 2**20, transcendentals=0),
        name="turn",
    )(*weights)


def add_rows(totals, rows):
    rows = rows.astype(f32).reshape(rows.shape[0] // 8, 8, M)
    return totals[0] + jnp.sum(rows, axis=0), totals[1] + jnp.sum(rows * rows, axis=0)


def early_sums_kernel(*refs):
    zero = jnp.zeros((8, M), f32)
    totals = zero, zero
    for piece in refs[:7]:
        for sub in range(NY):
            totals = add_rows(totals, piece[sub * PART1 : sub * PART1 + FIRST, :])
    for piece in refs[7:10]:
        for sub in range(NZ):
            totals = add_rows(totals, piece[sub * PART2 : (sub + 1) * PART2, :])
    refs[10][...], refs[11][...] = totals


def early_sums(pieces):
    return pl.pallas_call(
        early_sums_kernel,
        out_shape=(jax.ShapeDtypeStruct((8, M), f32),) * 2,
        in_specs=[VMEM] * 10,
        out_specs=(VMEM, VMEM),
        compiler_params=pltpu.CompilerParams(vmem_limit_bytes=VMEM_LIMIT),
        cost_estimate=pl.CostEstimate(
            flops=20 * D * M, bytes_accessed=6 * 2**20, transcendentals=0
        ),
        name="early_sums",
    )(*pieces)


def project_all_kernel(*refs):
    first, second = refs[:9], refs[9:14]
    sum_early, square_early, weights, k_gain, q_gain = refs[14:19]
    kv_out, q_out, hidden_out, held, normed, gains, gain_wide, w_held, sums, sems = refs[19:]
    y, z = position()
    copies = []
    for ref, place, begin, rows in piece_rows(first, NY * PART1):
        z_from = back_from(z, Z_OFF[place], NZ)
        for sub in range(rows // PART1):
            y_from = back_from(y, Y_OFF[begin // PART1 + sub], NY)
            block = y_from * NZ + z_from
            row = pl.multiple_of(block * BLOCK, 16)
            copies.append((ref.at[pl.ds(sub * PART1, FIRST)], held.at[pl.ds(row, FIRST)]))
            row = pl.multiple_of(block * GAIN_ROWS, 16)
            copies.append(
                (ref.at[pl.ds(sub * PART1 + FIRST, GAIN_ROWS)], gains.at[pl.ds(row, GAIN_ROWS)])
            )
    spans = [(second[0], 0, 0, 8), (second[1], 1, 0, 8), (second[2], 2, 0, 8)]
    spans += [(second[3], 3, 0, 4), (second[4], 3, 4, 4)]
    for ref, place, begin, count in spans:
        y_from = back_from(y, Y_OFF[place], NY)
        for sub in range(count):
            z_from = back_from(z, Z_OFF[begin + sub], NZ)
            row = pl.multiple_of((y_from * NZ + z_from) * BLOCK + FIRST, 16)
            copies.append((ref.at[pl.ds(sub * PART2, PART2)], held.at[pl.ds(row, PART2)]))
    for part in range(ROWS):
        copies.append((weights.at[part], w_held.at[part]))
    started = start_all(copies, sems)
    for copy in started[:-ROWS]:
        copy.wait()

    gain_rows = jnp.max(gains[:, :256].astype(f32).reshape(NY * NZ, GAIN_ROWS, 256), axis=1)
    gain_columns = gain_rows.T
    for block in range(NY * NZ):
        gain_wide[block * BLOCK : (block + 1) * BLOCK, :] = jnp.broadcast_to(
            gain_columns[:BLOCK, block : block + 1], (BLOCK, 128)
        )

    totals = sum_early[...], square_early[...]
    z_far, y_far = back_from(z, 4, NZ), back_from(y, 2, NY)
    late = [(y_from * NZ + z_far) * BLOCK for y_from in range(NY)]
    for row in late:
        totals = add_rows(totals, held[pl.ds(pl.multiple_of(row, 16), FIRST), :])
    late = [(y_far * NZ + z_from) * BLOCK + FIRST for z_from in range(NZ)]
    for row in late:
        totals = add_rows(totals, held[pl.ds(pl.multiple_of(row, 16), PART2), :])
    average = jnp.sum(totals[0], axis=0, keepdims=True) / D
    variance = jnp.sum(totals[1], axis=0, keepdims=True) / D - average * average
    scale = lax.rsqrt(variance + epsilon)
    for copy in started[-ROWS:]:
        copy.wait()

    chunk = 96
    for part in range(ROWS):
        for begin in range(part * DEEP, (part + 1) * DEEP, chunk):
            where = slice(begin, begin + chunk)
            gain = jnp.concatenate([gain_wide[where, :]] * 4, axis=1)
            rows = held[where, :].astype(f32)
            normed[where, :] = ((rows - average) * scale * gain).astype(bf16)
        product = jnp.dot(
            w_held[part], normed[part * DEEP : (part + 1) * DEEP, :], preferred_element_type=f32
        )
        if part == 0:
            sums[...] = product
        else:
            sums[...] += product
    kv_out[:HD, :] = head_norm(sums[:HD, :], k_gain[...]).astype(bf16)
    kv_out[HD:, :] = sums[HD:KV, :].astype(bf16)
    q_out[...] = head_norm(sums[KV : KV + HD, :], q_gain[...]).astype(bf16)
    hidden_out[...] = jax.nn.gelu(sums[KV + HD :, :]).astype(bf16)


def project_all(first, second, early, weights, k_gain, q_gain):
    copies = 64 + 32 + ROWS
    return pl.pallas_call(
        project_all_kernel,
        out_shape=(
            jax.ShapeDtypeStruct((KV, M), bf16),
            jax.ShapeDtypeStruct((HD, M), bf16),
            jax.ShapeDtypeStruct((FFL, M), bf16),
        ),
        in_specs=[ANY] * 14 + [VMEM] * 2 + [ANY] + [VMEM] * 2,
        out_specs=(VMEM, VMEM, VMEM),
        scratch_shapes=[
            pltpu.VMEM((D, M), bf16),
            pltpu.VMEM((D, M), bf16),
            pltpu.VMEM((NY * NZ * GAIN_ROWS, M), bf16),
            pltpu.VMEM((D, 128), f32),
            pltpu.VMEM((ROWS, KV + QU, DEEP), bf16),
            pltpu.VMEM((KV + QU, M), f32),
            pltpu.SemaphoreType.DMA((copies,)),
        ],
        compiler_params=pltpu.CompilerParams(vmem_limit_bytes=VMEM_LIMIT),
        cost_estimate=pl.CostEstimate(
            flops=2 * D * M * (KV + QU), bytes_accessed=18 * 2**20, transcendentals=FFL * M
        ),
        name="project_all",
    )(*first, *second, *early, weights, k_gain, q_gain)


def attend_kernel(*refs):
    pieces, query, out, scores = refs[:ROWS], refs[ROWS], refs[ROWS + 1], refs[ROWS + 2]
    largest = jnp.full((1, M), -jnp.inf, f32)
    for place, piece in enumerate(pieces):
        part = lax.dot_general(
            piece[:HD, :], query[...], (((0,), (0,)), ((), ())), preferred_element_type=f32
        ) * (1.0 / math.sqrt(HD))
        scores[place * M : (place + 1) * M, :] = part
        largest = jnp.maximum(largest, jnp.max(part, axis=0, keepdims=True))
    total = jnp.zeros((1, M), f32)
    for place in range(ROWS):
        part = jnp.exp(scores[place * M : (place + 1) * M, :] - largest)
        scores[place * M : (place + 1) * M, :] = part
        total = total + jnp.sum(part, axis=0, keepdims=True)
    share = 1.0 / total
    sums = jnp.zeros((HD, M), f32)
    for place, piece in enumerate(pieces):
        probs = (scores[place * M : (place + 1) * M, :] * share).astype(bf16)
        sums = sums + jnp.dot(piece[HD:, :], probs, preferred_element_type=f32)
    out[...] = sums.astype(bf16)


def attend(pieces, query):
    return pl.pallas_call(
        attend_kernel,
        out_shape=jax.ShapeDtypeStruct((HD, M), bf16),
        in_specs=[VMEM] * (ROWS + 1),
        out_specs=VMEM,
        scratch_shapes=[pltpu.VMEM((ROWS * M, M), f32)],
        compiler_params=pltpu.CompilerParams(vmem_limit_bytes=VMEM_LIMIT),
        cost_estimate=pl.CostEstimate(
            flops=20 * ROWS * M * M * HD, bytes_accessed=3 * 2**20, transcendentals=ROWS * M * M
        ),
        name="attend",
    )(*pieces, query)


def out_part_kernel(*refs):
    hidden, attended, weights, outs = refs[:9], refs[9:17], refs[17], refs[18:22]
    held, w_held, sems = refs[22:]
    y, z = position()
    copies = []
    for pieces, rows, first_row in ((hidden, FFL, 0), (attended, HD, DOWN_K)):
        for ref, place, begin, count in piece_rows(pieces, rows):
            z_from = back_from(z, Z_OFF[place], NZ)
            row = lax.div(z_from, 4) * OUT_ROWS + lax.rem(z_from, 4) * rows + (first_row + begin)
            copies.append((ref, held.at[pl.ds(pl.multiple_of(row, 16), count)]))
    for step in range(NY):
        x_from = lax.rem(2 * y + step, NX)
        for core in range(2):
            copies.append((weights.at[2 * x_from + core], w_held.at[2 * step + core]))
    started = start_all(copies, sems)
    for copy in started[:17]:
        copy.wait()
    for step in range(NY):
        started[17 + 2 * step].wait()
        started[18 + 2 * step].wait()
        total = jnp.dot(w_held[2 * step], held[:OUT_ROWS, :], preferred_element_type=f32)
        total = total + jnp.dot(
            w_held[2 * step + 1], held[OUT_ROWS:, :], preferred_element_type=f32
        )
        outs[step][...] = total.astype(outs[step].dtype)


def out_part(hidden, attended, weights):
    shape = (BLOCK, M)
    return pl.pallas_call(
        out_part_kernel,
        out_shape=(jax.ShapeDtypeStruct(shape, f32),) + (jax.ShapeDtypeStruct(shape, bf16),) * 3,
        in_specs=[ANY] * 18,
        out_specs=(VMEM,) * NY,
        scratch_shapes=[
            pltpu.VMEM((2 * OUT_ROWS, M), bf16),
            pltpu.VMEM((ROWS, BLOCK, OUT_ROWS), bf16),
            pltpu.SemaphoreType.DMA((17 + ROWS,)),
        ],
        compiler_params=pltpu.CompilerParams(vmem_limit_bytes=VMEM_LIMIT),
        cost_estimate=pl.CostEstimate(
            flops=4 * NY * BLOCK * M * OUT_ROWS, bytes_accessed=12 * 2**20, transcendentals=0
        ),
        name="out_part",
    )(*hidden, *attended, weights)


def after(value, *others):
    return lax.optimization_barrier((value, *others))[0]


def on_device(
    tokens,
    ln_gain,
    q_weight,
    k_weight,
    v_weight,
    up_weight,
    out_weight,
    down_weight,
    q_gain,
    k_gain,
):
    columns = tokens.T
    in_weights = turn(k_weight, v_weight, q_weight, up_weight)
    in_weights = lax.all_gather(in_weights, "row", axis=0, tiled=False)

    gain_tile = jnp.broadcast_to(jnp.pad(ln_gain, (0, M - BLOCK))[None, :], (GAIN_ROWS, M))
    part1 = jnp.concatenate([columns[:FIRST], gain_tile], axis=0)
    part1 = jnp.concatenate(
        [part1, along_col(part1, 1, 0), along_col(part1, -1, 0), along_col(part1, 2, 0)], axis=0
    )
    first = z_ring(part1, NY * PART1 // 2)
    part2 = jnp.concatenate(z_direct(columns[FIRST:]), axis=0)
    forth, back = along_col(part2, 1, 0), along_col(part2, -1, 0)
    half = NZ * PART2 // 2
    top, bottom = after(forth[:half], first[5], first[6]), after(back[half:], first[5], first[6])
    second = [part2, forth, back, along_col(top, 1, 0), along_col(bottom, -1, 0)]

    early = early_sums(first[:7] + second[:3])
    out_weights = jnp.concatenate([down_weight.T, out_weight.T], axis=1)
    pairs = [
        (
            (x * 2 + c) * NY * NZ + y * NZ + z,
            (((x + y) % NX) * 2 + c) * NY * NZ + x * NZ + z,
        )
        for x in range(NX)
        for c in range(2)
        for y in range(NY)
        for z in range(NZ)
    ]
    out_weights = lax.ppermute(out_weights, ("row", "col"), pairs)

    wide = lambda gain: jnp.broadcast_to(gain.reshape(HD, 1), (HD, M))
    out_weights = after(out_weights, part2, first[3], first[4])
    k_wide = after(wide(k_gain), out_weights)
    out_weights = lax.all_gather(out_weights, "row", axis=0, tiled=False)
    own_kv, query, hidden = project_all(first, second, early, in_weights, k_wide, wide(q_gain))
    kv = [own_kv, along_row(own_kv, 1, 0), along_row(own_kv, -1, 0), along_row(own_kv, 2, 0)]
    kv += [along_row(piece, 0, 1) for piece in kv]
    hidden = z_ring(hidden, FFL // 2)
    attended = attend(kv, query)
    parts = out_part(hidden, z_ring(attended), out_weights)
    summed = columns.astype(f32) + parts[0]
    for step in range(1, NY):
        summed = summed + along_col(parts[step], step, 0).astype(f32)
    return summed.astype(bf16).T


def solution(mesh):
    return jax.shard_map(
        on_device,
        mesh=mesh,
        in_specs=(
            P("row", "col"),
            P("col"),
            P("row", "col"),
            P("row", "col"),
            P("row", "col"),
            P("row", "col"),
            P("row", "col"),
            P("row", "col"),
            P("col", None),
            P("col", None),
        ),
        out_specs=P("row", "col"),
        check_vma=False,
    )
```

```python
import math

import jax
import jax.numpy as jnp
from jax import lax
from jax.experimental import pallas as pl
from jax.experimental.pallas import tpu as pltpu
from jax.sharding import PartitionSpec as P

D = 6144
HD = 128
NX, NY, NZ = 4, 4, 8
ROWS = 2 * NX
M = 512
BLOCK = D // (NY * NZ)
FIRST = 96
GAIN_ROWS = 16
PART1 = FIRST + GAIN_ROWS
PART2 = BLOCK - FIRST
DEEP = D // ROWS
FFL = 384
KV = 2 * HD
QU = HD + FFL
OUT_K = 512
DOWN_K = 1536
OUT_ROWS = DOWN_K + OUT_K
Y_OFF = (0, 1, 3, 2)
Z_OFF = (0, 1, 7, 2, 6, 3, 5, 4)
epsilon = 1e-06
f32, bf16 = jnp.float32, jnp.bfloat16
MIB = 1024 * 1024
ANY = pl.BlockSpec(memory_space=pl.ANY)
VMEM = pl.BlockSpec(memory_space=pltpu.VMEM)


def along_col(value, dy, dz):
    pairs = [
        (y * NZ + z, ((y + dy) % NY) * NZ + (z + dz) % NZ) for y in range(NY) for z in range(NZ)
    ]
    return lax.ppermute(value, "col", pairs)


def along_row(value, dx, dc):
    pairs = [
        (x * 2 + c, ((x + dx) % NX) * 2 + (c + dc) % 2) for x in range(NX) for c in range(2)
    ]
    return lax.ppermute(value, "row", pairs)


def z_ring(block, half=None):
    blocks = z_ring_first(block)
    return blocks + z_ring_last(blocks[3], blocks[4], half)


def z_ring_first(block):
    one, other = along_col(block, 0, 1), along_col(block, 0, -1)
    return [block, one, other, along_col(one, 0, 1), along_col(other, 0, -1)]


def z_ring_last(forth, back, half=None):
    forth, back = along_col(forth, 0, 1), along_col(back, 0, -1)
    if half is None:
        return [forth, back, along_col(forth, 0, 1)]
    return [forth, back, along_col(forth[:half], 0, 1), along_col(back[half:], 0, -1)]


def position():
    col = lax.axis_index("col")
    return lax.div(col, NZ), lax.rem(col, NZ)


def back_from(index, offset, size):
    return lax.rem(index + (size - offset), size)


def start_all(copies, sems):
    started = []
    for number, (source, target) in enumerate(copies):
        copy = pltpu.make_async_copy(source, target, sems.at[number])
        copy.start()
        started.append(copy)
    return started


def head_norm(values, gain):
    gain = jnp.concatenate([jnp.broadcast_to(gain, (HD, HD)).T] * (M // HD), axis=1)
    average = jnp.mean(values, axis=0, keepdims=True)
    variance = jnp.mean(values * values, axis=0, keepdims=True) - average * average
    return (values - average) * lax.rsqrt(variance + epsilon) * gain


def piece_rows(refs, rows):
    spans = [(ref, place, 0, rows) for place, ref in enumerate(refs[:7])]
    if len(refs) == 8:
        return spans + [(refs[7], 7, 0, rows)]
    half = refs[7].shape[0]
    return spans + [(refs[7], 7, 0, half), (refs[8], 7, half, rows - half)]


def turn_kernel(k_weight, v_weight, q_weight, up_weight, out):
    begin = 0
    for weight in (k_weight, v_weight, q_weight, up_weight):
        for step in range(weight.shape[1] // HD):
            columns = weight[:, step * HD : (step + 1) * HD]
            out[begin : begin + HD, :] = columns.T
            begin += HD


def turn(*weights):
    return pl.pallas_call(
        turn_kernel,
        out_shape=jax.ShapeDtypeStruct((KV + QU, DEEP), bf16),
        in_specs=[VMEM] * 4,
        out_specs=VMEM,
        compiler_params=pltpu.CompilerParams(vmem_limit_bytes=56 * MIB),
        cost_estimate=pl.CostEstimate(flops=0, bytes_accessed=3 * 2**20, transcendentals=0),
        name="turn",
    )(*weights)


def add_rows(totals, rows):
    rows = rows.astype(f32).reshape(rows.shape[0] // 8, 8, M)
    return totals[0] + jnp.sum(rows, axis=0), totals[1] + jnp.sum(rows * rows, axis=0)


def early_sums_kernel(*refs):
    zero = jnp.zeros((8, M), f32)
    totals = zero, zero
    for piece in refs[:7]:
        for sub in range(NY):
            totals = add_rows(totals, piece[sub * PART1 : sub * PART1 + FIRST, :])
    for piece in refs[7:10]:
        for sub in range(NZ):
            totals = add_rows(totals, piece[sub * PART2 : (sub + 1) * PART2, :])
    refs[10][...], refs[11][...] = totals


def early_sums(pieces):
    return pl.pallas_call(
        early_sums_kernel,
        out_shape=(jax.ShapeDtypeStruct((8, M), f32),) * 2,
        in_specs=[VMEM] * 10,
        out_specs=(VMEM, VMEM),
        compiler_params=pltpu.CompilerParams(vmem_limit_bytes=16 * MIB),
        cost_estimate=pl.CostEstimate(
            flops=20 * D * M, bytes_accessed=6 * 2**20, transcendentals=0
        ),
        name="early_sums",
    )(*pieces)


def project_all_kernel(*refs):
    first, second = refs[:9], refs[9:14]
    sum_early, square_early, weights, k_gain, q_gain = refs[14:19]
    kv_out, q_out, hidden_out, held, normed, gains, gain_wide, w_held, sums, sems = refs[19:]
    y, z = position()
    copies = []
    for ref, place, begin, rows in piece_rows(first, NY * PART1):
        z_from = back_from(z, Z_OFF[place], NZ)
        for sub in range(rows // PART1):
            y_from = back_from(y, Y_OFF[begin // PART1 + sub], NY)
            block = y_from * NZ + z_from
            row = pl.multiple_of(block * BLOCK, 16)
            copies.append((ref.at[pl.ds(sub * PART1, FIRST)], held.at[pl.ds(row, FIRST)]))
            row = pl.multiple_of(block * GAIN_ROWS, 16)
            copies.append(
                (ref.at[pl.ds(sub * PART1 + FIRST, GAIN_ROWS)], gains.at[pl.ds(row, GAIN_ROWS)])
            )
    spans = [(second[0], 0, 0, 8), (second[1], 1, 0, 8), (second[2], 2, 0, 8)]
    spans += [(second[3], 3, 0, 4), (second[4], 3, 4, 4)]
    for ref, place, begin, count in spans:
        y_from = back_from(y, Y_OFF[place], NY)
        for sub in range(count):
            z_from = back_from(z, Z_OFF[begin + sub], NZ)
            row = pl.multiple_of((y_from * NZ + z_from) * BLOCK + FIRST, 16)
            copies.append((ref.at[pl.ds(sub * PART2, PART2)], held.at[pl.ds(row, PART2)]))
    for part in range(ROWS):
        copies.append((weights.at[part], w_held.at[part]))
    started = start_all(copies, sems)
    for copy in started[:-ROWS]:
        copy.wait()

    gain_rows = jnp.max(gains[:, :256].astype(f32).reshape(NY * NZ, GAIN_ROWS, 256), axis=1)
    gain_columns = gain_rows.T
    for block in range(NY * NZ):
        gain_wide[block * BLOCK : (block + 1) * BLOCK, :] = jnp.broadcast_to(
            gain_columns[:BLOCK, block : block + 1], (BLOCK, 128)
        )

    totals = sum_early[...], square_early[...]
    z_far, y_far = back_from(z, 4, NZ), back_from(y, 2, NY)
    late = [(y_from * NZ + z_far) * BLOCK for y_from in range(NY)]
    for row in late:
        totals = add_rows(totals, held[pl.ds(pl.multiple_of(row, 16), FIRST), :])
    late = [(y_far * NZ + z_from) * BLOCK + FIRST for z_from in range(NZ)]
    for row in late:
        totals = add_rows(totals, held[pl.ds(pl.multiple_of(row, 16), PART2), :])
    average = jnp.sum(totals[0], axis=0, keepdims=True) / D
    variance = jnp.sum(totals[1], axis=0, keepdims=True) / D - average * average
    scale = lax.rsqrt(variance + epsilon)
    for copy in started[-ROWS:]:
        copy.wait()

    chunk = 96
    for part in range(ROWS):
        for begin in range(part * DEEP, (part + 1) * DEEP, chunk):
            where = slice(begin, begin + chunk)
            gain = jnp.concatenate([gain_wide[where, :]] * 4, axis=1)
            rows = held[where, :].astype(f32)
            normed[where, :] = ((rows - average) * scale * gain).astype(bf16)
        product = jnp.dot(
            w_held[part], normed[part * DEEP : (part + 1) * DEEP, :], preferred_element_type=f32
        )
        if part == 0:
            sums[...] = product
        else:
            sums[...] += product
    kv_out[:HD, :] = head_norm(sums[:HD, :], k_gain[...]).astype(bf16)
    kv_out[HD:, :] = sums[HD:KV, :].astype(bf16)
    q_out[...] = head_norm(sums[KV : KV + HD, :], q_gain[...]).astype(bf16)
    hidden_out[...] = jax.nn.gelu(sums[KV + HD :, :]).astype(bf16)


def project_all(first, second, early, weights, k_gain, q_gain):
    copies = 64 + 32 + ROWS
    return pl.pallas_call(
        project_all_kernel,
        out_shape=(
            jax.ShapeDtypeStruct((KV, M), bf16),
            jax.ShapeDtypeStruct((HD, M), bf16),
            jax.ShapeDtypeStruct((FFL, M), bf16),
        ),
        in_specs=[ANY] * 14 + [VMEM] * 2 + [ANY] + [VMEM] * 2,
        out_specs=(VMEM, VMEM, VMEM),
        scratch_shapes=[
            pltpu.VMEM((D, M), bf16),
            pltpu.VMEM((D, M), bf16),
            pltpu.VMEM((NY * NZ * GAIN_ROWS, M), bf16),
            pltpu.VMEM((D, 128), f32),
            pltpu.VMEM((ROWS, KV + QU, DEEP), bf16),
            pltpu.VMEM((KV + QU, M), f32),
            pltpu.SemaphoreType.DMA((copies,)),
        ],
        compiler_params=pltpu.CompilerParams(vmem_limit_bytes=56 * MIB),
        cost_estimate=pl.CostEstimate(
            flops=2 * D * M * (KV + QU), bytes_accessed=18 * 2**20, transcendentals=FFL * M
        ),
        name="project_all",
    )(*first, *second, *early, weights, k_gain, q_gain)


def attend_kernel(*refs):
    pieces, query, out, scores = refs[:ROWS], refs[ROWS], refs[ROWS + 1], refs[ROWS + 2]
    largest = jnp.full((1, M), -jnp.inf, f32)
    for place, piece in enumerate(pieces):
        part = lax.dot_general(
            piece[:HD, :], query[...], (((0,), (0,)), ((), ())), preferred_element_type=f32
        ) * (1.0 / math.sqrt(HD))
        scores[place * M : (place + 1) * M, :] = part
        largest = jnp.maximum(largest, jnp.max(part, axis=0, keepdims=True))
    total = jnp.zeros((1, M), f32)
    for place in range(ROWS):
        part = jnp.exp(scores[place * M : (place + 1) * M, :] - largest)
        scores[place * M : (place + 1) * M, :] = part
        total = total + jnp.sum(part, axis=0, keepdims=True)
    share = 1.0 / total
    sums = jnp.zeros((HD, M), f32)
    for place, piece in enumerate(pieces):
        probs = (scores[place * M : (place + 1) * M, :] * share).astype(bf16)
        sums = sums + jnp.dot(piece[HD:, :], probs, preferred_element_type=f32)
    out[...] = sums.astype(bf16)


def attend(pieces, query):
    return pl.pallas_call(
        attend_kernel,
        out_shape=jax.ShapeDtypeStruct((HD, M), bf16),
        in_specs=[VMEM] * (ROWS + 1),
        out_specs=VMEM,
        scratch_shapes=[pltpu.VMEM((ROWS * M, M), f32)],
        compiler_params=pltpu.CompilerParams(vmem_limit_bytes=20 * MIB),
        cost_estimate=pl.CostEstimate(
            flops=20 * ROWS * M * M * HD, bytes_accessed=3 * 2**20, transcendentals=ROWS * M * M
        ),
        name="attend",
    )(*pieces, query)


def out_part_kernel(*refs):
    hidden, attended, weights, outs = refs[:9], refs[9:17], refs[17], refs[18:22]
    held, w_held, sems = refs[22:]
    y, z = position()
    copies = []
    for pieces, rows, first_row in ((hidden, FFL, 0), (attended, HD, DOWN_K)):
        for ref, place, begin, count in piece_rows(pieces, rows):
            z_from = back_from(z, Z_OFF[place], NZ)
            row = lax.div(z_from, 4) * OUT_ROWS + lax.rem(z_from, 4) * rows + (first_row + begin)
            copies.append((ref, held.at[pl.ds(pl.multiple_of(row, 16), count)]))
    for step in range(NY):
        x_from = lax.rem(2 * y + step, NX)
        for core in range(2):
            copies.append((weights.at[2 * x_from + core], w_held.at[2 * step + core]))
    started = start_all(copies, sems)
    for copy in started[:17]:
        copy.wait()
    for step in range(NY):
        started[17 + 2 * step].wait()
        started[18 + 2 * step].wait()
        total = jnp.dot(w_held[2 * step], held[:OUT_ROWS, :], preferred_element_type=f32)
        total = total + jnp.dot(
            w_held[2 * step + 1], held[OUT_ROWS:, :], preferred_element_type=f32
        )
        outs[step][...] = total.astype(outs[step].dtype)


def out_part(hidden, attended, weights):
    shape = (BLOCK, M)
    return pl.pallas_call(
        out_part_kernel,
        out_shape=(jax.ShapeDtypeStruct(shape, f32),) + (jax.ShapeDtypeStruct(shape, bf16),) * 3,
        in_specs=[ANY] * 18,
        out_specs=(VMEM,) * NY,
        scratch_shapes=[
            pltpu.VMEM((2 * OUT_ROWS, M), bf16),
            pltpu.VMEM((ROWS, BLOCK, OUT_ROWS), bf16),
            pltpu.SemaphoreType.DMA((17 + ROWS,)),
        ],
        compiler_params=pltpu.CompilerParams(vmem_limit_bytes=56 * MIB),
        cost_estimate=pl.CostEstimate(
            flops=4 * NY * BLOCK * M * OUT_ROWS, bytes_accessed=12 * 2**20, transcendentals=0
        ),
        name="out_part",
    )(*hidden, *attended, weights)


def after(value, *others):
    return lax.optimization_barrier((value, *others))[0]


def on_device(
    tokens,
    ln_gain,
    q_weight,
    k_weight,
    v_weight,
    up_weight,
    out_weight,
    down_weight,
    q_gain,
    k_gain,
):
    columns = tokens.T
    in_weights = turn(k_weight, v_weight, q_weight, up_weight)
    in_weights = lax.all_gather(in_weights, "row", axis=0, tiled=False)

    gain_tile = jnp.broadcast_to(jnp.pad(ln_gain, (0, M - BLOCK))[None, :], (GAIN_ROWS, M))
    part1 = jnp.concatenate([columns[:FIRST], gain_tile], axis=0)
    part2 = z_ring(columns[FIRST:])
    part1 = jnp.concatenate(
        [part1, along_col(part1, 1, 0), along_col(part1, -1, 0), along_col(part1, 2, 0)], axis=0
    )
    first = z_ring(part1, NY * PART1 // 2)
    part2 = after(jnp.concatenate(part2, axis=0), first[1], first[2])
    forth, back = along_col(part2, 1, 0), along_col(part2, -1, 0)
    half = NZ * PART2 // 2
    top, bottom = after(forth[:half], first[5], first[6]), after(back[half:], first[5], first[6])
    second = [part2, forth, back, along_col(top, 1, 0), along_col(bottom, -1, 0)]

    early = early_sums(first[:7] + second[:3])
    out_weights = jnp.concatenate([down_weight.T, out_weight.T], axis=1)
    pairs = [
        (
            (x * 2 + c) * NY * NZ + y * NZ + z,
            (((x + y) % NX) * 2 + c) * NY * NZ + x * NZ + z,
        )
        for x in range(NX)
        for c in range(2)
        for y in range(NY)
        for z in range(NZ)
    ]
    out_weights = after(out_weights, *first[7:], *second[3:], *early)
    out_weights = lax.ppermute(out_weights, ("row", "col"), pairs)

    own_kv, query, hidden = project_all(first, second, early, in_weights, k_gain, q_gain)
    kv = [own_kv, along_row(own_kv, 1, 0), along_row(own_kv, -1, 0), along_row(own_kv, 2, 0)]
    kv += [along_row(piece, 0, 1) for piece in (after(own_kv, *kv[1:]), *kv[1:])]
    hidden = z_ring_first(hidden)
    out_weights = after(out_weights, *kv[1:], hidden[1], hidden[2])
    out_weights = lax.all_gather(out_weights, "row", axis=0, tiled=False)
    attended = attend(kv, after(query, hidden[1], hidden[2]))
    attended = z_ring(attended)
    forth, back = (after(block, attended[1], attended[2]) for block in hidden[3:])
    hidden += z_ring_last(forth, back, FFL // 2)
    parts = out_part(hidden, attended, out_weights)
    summed = columns.astype(f32) + parts[0]
    for step in range(1, NY):
        summed = summed + along_col(parts[step], step, 0).astype(f32)
    return summed.astype(bf16).T


def solution(mesh):
    return jax.shard_map(
        on_device,
        mesh=mesh,
        in_specs=(
            P("row", "col"),
            P("col"),
            P("row", "col"),
            P("row", "col"),
            P("row", "col"),
            P("row", "col"),
            P("row", "col"),
            P("row", "col"),
            P("col", None),
            P("col", None),
        ),
        out_specs=P("row", "col"),
        check_vma=False,
    )
```

```python
import functools
import math

import jax
import jax.numpy as jnp
from jax import lax
from jax.experimental import pallas as pl
from jax.experimental.pallas import tpu as pltpu
from jax.sharding import PartitionSpec as P

D = 6144
HD = 128
NX, NY, NZ = 4, 4, 8
ROWS = 2 * NX
M = 512
BLOCK = D // (NY * NZ)
FIRST = 96
GAIN_ROWS = 16
PART1 = FIRST + GAIN_ROWS
PART2 = BLOCK - FIRST
DEEP = D // ROWS
FFL = 384
KV = 2 * HD
QU = HD + FFL
OUT_K = 512
DOWN_K = 1536
OUT_ROWS = DOWN_K + OUT_K
Y_OFF = (0, 1, 3, 2)
Z_OFF = (0, 1, 7, 2, 6, 3, 5, 4)
epsilon = 1e-06
f32, bf16 = jnp.float32, jnp.bfloat16
MIB = 1024 * 1024
ANY = pl.BlockSpec(memory_space=pl.ANY)
VMEM = pl.BlockSpec(memory_space=pltpu.VMEM)


def along_col(value, dy, dz):
    pairs = [
        (y * NZ + z, ((y + dy) % NY) * NZ + (z + dz) % NZ) for y in range(NY) for z in range(NZ)
    ]
    return lax.ppermute(value, "col", pairs)


def along_row(value, dx, dc):
    pairs = [
        (x * 2 + c, ((x + dx) % NX) * 2 + (c + dc) % 2) for x in range(NX) for c in range(2)
    ]
    return lax.ppermute(value, "row", pairs)


def z_ring(block, half=None):
    blocks = z_ring_first(block)
    return blocks + z_ring_last(blocks[3], blocks[4], half)


def z_ring_first(block):
    one, other = along_col(block, 0, 1), along_col(block, 0, -1)
    return [block, one, other, along_col(one, 0, 1), along_col(other, 0, -1)]


def z_ring_last(forth, back, half=None):
    forth, back = along_col(forth, 0, 1), along_col(back, 0, -1)
    if half is None:
        return [forth, back, along_col(forth, 0, 1)]
    return [forth, back, along_col(forth[:half], 0, 1), along_col(back[half:], 0, -1)]


def turn_over(block, shift):
    pairs = [
        (
            (x * 2 + c) * NY * NZ + y * NZ + z,
            (((x + y + shift) % NX) * 2 + c) * NY * NZ + x * NZ + z,
        )
        for x in range(NX)
        for c in range(2)
        for y in range(NY)
        for z in range(NZ)
    ]
    return lax.ppermute(block, ("row", "col"), pairs)


def position():
    col = lax.axis_index("col")
    return lax.div(col, NZ), lax.rem(col, NZ)


def back_from(index, offset, size):
    return lax.rem(index + (size - offset), size)


def start_all(copies, sems):
    started = []
    for number, (source, target) in enumerate(copies):
        copy = pltpu.make_async_copy(source, target, sems.at[number])
        copy.start()
        started.append(copy)
    return started


def head_norm(values, gain):
    gain = jnp.concatenate([jnp.broadcast_to(gain, (HD, HD)).T] * (M // HD), axis=1)
    average = jnp.mean(values, axis=0, keepdims=True)
    variance = jnp.mean(values * values, axis=0, keepdims=True) - average * average
    return (values - average) * lax.rsqrt(variance + epsilon) * gain


def piece_rows(refs, rows):
    spans = [(ref, place, 0, rows) for place, ref in enumerate(refs[:7])]
    if len(refs) == 8:
        return spans + [(refs[7], 7, 0, rows)]
    half = refs[7].shape[0]
    return spans + [(refs[7], 7, 0, half), (refs[8], 7, half, rows - half)]


def turn_kernel(k_weight, v_weight, q_weight, up_weight, out):
    begin = 0
    for weight in (k_weight, v_weight, q_weight, up_weight):
        for step in range(weight.shape[1] // HD):
            columns = weight[:, step * HD : (step + 1) * HD]
            out[begin : begin + HD, :] = columns.T
            begin += HD


def turn(*weights):
    return pl.pallas_call(
        turn_kernel,
        out_shape=jax.ShapeDtypeStruct((KV + QU, DEEP), bf16),
        in_specs=[VMEM] * 4,
        out_specs=VMEM,
        compiler_params=pltpu.CompilerParams(vmem_limit_bytes=56 * MIB),
        cost_estimate=pl.CostEstimate(flops=0, bytes_accessed=3 * 2**20, transcendentals=0),
        name="turn",
    )(*weights)


def add_rows(totals, rows):
    rows = rows.astype(f32).reshape(rows.shape[0] // 8, 8, M)
    return totals[0] + jnp.sum(rows, axis=0), totals[1] + jnp.sum(rows * rows, axis=0)


def early_sums_kernel(*refs):
    zero = jnp.zeros((8, M), f32)
    totals = zero, zero
    for piece in refs[:7]:
        for sub in range(NY):
            totals = add_rows(totals, piece[sub * PART1 : sub * PART1 + FIRST, :])
    for piece in refs[7:10]:
        for sub in range(NZ):
            totals = add_rows(totals, piece[sub * PART2 : (sub + 1) * PART2, :])
    refs[10][...], refs[11][...] = totals


def early_sums(pieces):
    return pl.pallas_call(
        early_sums_kernel,
        out_shape=(jax.ShapeDtypeStruct((8, M), f32),) * 2,
        in_specs=[VMEM] * 10,
        out_specs=(VMEM, VMEM),
        compiler_params=pltpu.CompilerParams(vmem_limit_bytes=16 * MIB),
        cost_estimate=pl.CostEstimate(
            flops=20 * D * M, bytes_accessed=6 * 2**20, transcendentals=0
        ),
        name="early_sums",
    )(*pieces)


def project_all_kernel(*refs):
    first, second = refs[:9], refs[9:14]
    sum_early, square_early, weights, k_gain, q_gain = refs[14:19]
    kv_out, q_out, hidden_out, held, normed, gains, gain_wide, w_held, sums, sems = refs[19:]
    y, z = position()
    copies = []
    for ref, place, begin, rows in piece_rows(first, NY * PART1):
        z_from = back_from(z, Z_OFF[place], NZ)
        for sub in range(rows // PART1):
            y_from = back_from(y, Y_OFF[begin // PART1 + sub], NY)
            block = y_from * NZ + z_from
            row = pl.multiple_of(block * BLOCK, 16)
            copies.append((ref.at[pl.ds(sub * PART1, FIRST)], held.at[pl.ds(row, FIRST)]))
            row = pl.multiple_of(block * GAIN_ROWS, 16)
            copies.append(
                (ref.at[pl.ds(sub * PART1 + FIRST, GAIN_ROWS)], gains.at[pl.ds(row, GAIN_ROWS)])
            )
    spans = [(second[0], 0, 0, 8), (second[1], 1, 0, 8), (second[2], 2, 0, 8)]
    spans += [(second[3], 3, 0, 4), (second[4], 3, 4, 4)]
    for ref, place, begin, count in spans:
        y_from = back_from(y, Y_OFF[place], NY)
        for sub in range(count):
            z_from = back_from(z, Z_OFF[begin + sub], NZ)
            row = pl.multiple_of((y_from * NZ + z_from) * BLOCK + FIRST, 16)
            copies.append((ref.at[pl.ds(sub * PART2, PART2)], held.at[pl.ds(row, PART2)]))
    for part in range(ROWS):
        copies.append((weights.at[part], w_held.at[part]))
    started = start_all(copies, sems)
    for copy in started[:-ROWS]:
        copy.wait()

    gain_rows = jnp.max(gains[:, :256].astype(f32).reshape(NY * NZ, GAIN_ROWS, 256), axis=1)
    gain_columns = gain_rows.T
    for block in range(NY * NZ):
        gain_wide[block * BLOCK : (block + 1) * BLOCK, :] = jnp.broadcast_to(
            gain_columns[:BLOCK, block : block + 1], (BLOCK, 128)
        )

    totals = sum_early[...], square_early[...]
    z_far, y_far = back_from(z, 4, NZ), back_from(y, 2, NY)
    late = [(y_from * NZ + z_far) * BLOCK for y_from in range(NY)]
    for row in late:
        totals = add_rows(totals, held[pl.ds(pl.multiple_of(row, 16), FIRST), :])
    late = [(y_far * NZ + z_from) * BLOCK + FIRST for z_from in range(NZ)]
    for row in late:
        totals = add_rows(totals, held[pl.ds(pl.multiple_of(row, 16), PART2), :])
    average = jnp.sum(totals[0], axis=0, keepdims=True) / D
    variance = jnp.sum(totals[1], axis=0, keepdims=True) / D - average * average
    scale = lax.rsqrt(variance + epsilon)
    for copy in started[-ROWS:]:
        copy.wait()

    chunk = 96
    for part in range(ROWS):
        for begin in range(part * DEEP, (part + 1) * DEEP, chunk):
            where = slice(begin, begin + chunk)
            gain = jnp.concatenate([gain_wide[where, :]] * 4, axis=1)
            rows = held[where, :].astype(f32)
            normed[where, :] = ((rows - average) * scale * gain).astype(bf16)
        product = jnp.dot(
            w_held[part], normed[part * DEEP : (part + 1) * DEEP, :], preferred_element_type=f32
        )
        if part == 0:
            sums[...] = product
        else:
            sums[...] += product
    kv_out[:HD, :] = head_norm(sums[:HD, :], k_gain[...]).astype(bf16)
    kv_out[HD:, :] = sums[HD:KV, :].astype(bf16)
    q_out[...] = head_norm(sums[KV : KV + HD, :], q_gain[...]).astype(bf16)
    hidden_out[...] = jax.nn.gelu(sums[KV + HD :, :]).astype(bf16)


def project_all(first, second, early, weights, k_gain, q_gain):
    copies = 64 + 32 + ROWS
    return pl.pallas_call(
        project_all_kernel,
        out_shape=(
            jax.ShapeDtypeStruct((KV, M), bf16),
            jax.ShapeDtypeStruct((HD, M), bf16),
            jax.ShapeDtypeStruct((FFL, M), bf16),
        ),
        in_specs=[ANY] * 14 + [VMEM] * 2 + [ANY] + [VMEM] * 2,
        out_specs=(VMEM, VMEM, VMEM),
        scratch_shapes=[
            pltpu.VMEM((D, M), bf16),
            pltpu.VMEM((D, M), bf16),
            pltpu.VMEM((NY * NZ * GAIN_ROWS, M), bf16),
            pltpu.VMEM((D, 128), f32),
            pltpu.VMEM((ROWS, KV + QU, DEEP), bf16),
            pltpu.VMEM((KV + QU, M), f32),
            pltpu.SemaphoreType.DMA((copies,)),
        ],
        compiler_params=pltpu.CompilerParams(vmem_limit_bytes=56 * MIB),
        cost_estimate=pl.CostEstimate(
            flops=2 * D * M * (KV + QU), bytes_accessed=18 * 2**20, transcendentals=FFL * M
        ),
        name="project_all",
    )(*first, *second, *early, weights, k_gain, q_gain)


def attend_kernel(*refs):
    pieces, query, out, scores = refs[:ROWS], refs[ROWS], refs[ROWS + 1], refs[ROWS + 2]
    largest = jnp.full((1, M), -jnp.inf, f32)
    for place, piece in enumerate(pieces):
        part = lax.dot_general(
            piece[:HD, :], query[...], (((0,), (0,)), ((), ())), preferred_element_type=f32
        ) * (1.0 / math.sqrt(HD))
        scores[place * M : (place + 1) * M, :] = part
        largest = jnp.maximum(largest, jnp.max(part, axis=0, keepdims=True))
    total = jnp.zeros((1, M), f32)
    for place in range(ROWS):
        part = jnp.exp(scores[place * M : (place + 1) * M, :] - largest)
        scores[place * M : (place + 1) * M, :] = part
        total = total + jnp.sum(part, axis=0, keepdims=True)
    share = 1.0 / total
    sums = jnp.zeros((HD, M), f32)
    for place, piece in enumerate(pieces):
        probs = (scores[place * M : (place + 1) * M, :] * share).astype(bf16)
        sums = sums + jnp.dot(piece[HD:, :], probs, preferred_element_type=f32)
    out[...] = sums.astype(bf16)


def attend(pieces, query):
    return pl.pallas_call(
        attend_kernel,
        out_shape=jax.ShapeDtypeStruct((HD, M), bf16),
        in_specs=[VMEM] * (ROWS + 1),
        out_specs=VMEM,
        scratch_shapes=[pltpu.VMEM((ROWS * M, M), f32)],
        compiler_params=pltpu.CompilerParams(vmem_limit_bytes=20 * MIB),
        cost_estimate=pl.CostEstimate(
            flops=20 * ROWS * M * M * HD, bytes_accessed=3 * 2**20, transcendentals=ROWS * M * M
        ),
        name="attend",
    )(*pieces, query)


def out_part_kernel(steps, *refs):
    hidden, attended, weights, outs = refs[:9], refs[9:17], refs[17], refs[18 : 18 + len(steps)]
    held, w_held, sems = refs[18 + len(steps) :]
    y, z = position()
    copies = []
    for pieces, rows, first_row in ((hidden, FFL, 0), (attended, HD, DOWN_K)):
        for ref, place, begin, count in piece_rows(pieces, rows):
            z_from = back_from(z, Z_OFF[place], NZ)
            row = lax.div(z_from, 4) * OUT_ROWS + lax.rem(z_from, 4) * rows + (first_row + begin)
            copies.append((ref, held.at[pl.ds(pl.multiple_of(row, 16), count)]))
    half = BLOCK // 2
    for place, step in enumerate(steps):
        for core in range(2):
            for part in range(2):
                source = weights.at[2 * lax.rem(2 * y + step + part, NX) + core]
                rows = pl.ds(part * half, half)
                copies.append((source.at[rows], w_held.at[2 * place + core].at[rows]))
    started = start_all(copies, sems)
    for copy in started[:17]:
        copy.wait()
    for place in range(len(steps)):
        for copy in started[17 + 4 * place : 21 + 4 * place]:
            copy.wait()
        total = jnp.dot(w_held[2 * place], held[:OUT_ROWS, :], preferred_element_type=f32)
        total = total + jnp.dot(
            w_held[2 * place + 1], held[OUT_ROWS:, :], preferred_element_type=f32
        )
        outs[place][...] = total.astype(outs[place].dtype)


def out_part(steps, kind, hidden, attended, weights):
    count = len(steps)
    return pl.pallas_call(
        functools.partial(out_part_kernel, steps),
        out_shape=(jax.ShapeDtypeStruct((BLOCK, M), kind),) * count,
        in_specs=[ANY] * 18,
        out_specs=(VMEM,) * count,
        scratch_shapes=[
            pltpu.VMEM((2 * OUT_ROWS, M), bf16),
            pltpu.VMEM((2 * count, BLOCK, OUT_ROWS), bf16),
            pltpu.SemaphoreType.DMA((17 + 4 * count,)),
        ],
        compiler_params=pltpu.CompilerParams(vmem_limit_bytes=56 * MIB),
        cost_estimate=pl.CostEstimate(
            flops=4 * count * BLOCK * M * OUT_ROWS,
            bytes_accessed=(4 + 2 * count) * 2**20,
            transcendentals=0,
        ),
        name="out_part",
    )(*hidden, *attended, weights)


def after(value, *others):
    return lax.optimization_barrier((value, *others))[0]


def on_device(
    tokens,
    ln_gain,
    q_weight,
    k_weight,
    v_weight,
    up_weight,
    out_weight,
    down_weight,
    q_gain,
    k_gain,
):
    columns = tokens.T
    in_weights = turn(k_weight, v_weight, q_weight, up_weight)
    in_weights = lax.all_gather(in_weights, "row", axis=0, tiled=False)

    gain_tile = jnp.broadcast_to(jnp.pad(ln_gain, (0, M - BLOCK))[None, :], (GAIN_ROWS, M))
    part1 = jnp.concatenate([columns[:FIRST], gain_tile], axis=0)
    part2 = z_ring(columns[FIRST:])
    part1 = jnp.concatenate(
        [part1, along_col(part1, 1, 0), along_col(part1, -1, 0), along_col(part1, 2, 0)], axis=0
    )
    first = z_ring(part1, NY * PART1 // 2)
    part2 = after(jnp.concatenate(part2, axis=0), first[1], first[2])
    forth, back = along_col(part2, 1, 0), along_col(part2, -1, 0)
    half = NZ * PART2 // 2
    top, bottom = after(forth[:half], first[5], first[6]), after(back[half:], first[5], first[6])
    second = [part2, forth, back, along_col(top, 1, 0), along_col(bottom, -1, 0)]

    early = early_sums(first[:7] + second[:3])
    out_weights = jnp.concatenate([down_weight.T, out_weight.T], axis=1)
    out_weights = after(out_weights, *first[7:], *second[3:], *early)
    half = BLOCK // 2
    top, bottom = turn_over(out_weights[:half], 0), turn_over(out_weights[half:], 1)

    own_kv, query, hidden = project_all(first, second, early, in_weights, k_gain, q_gain)
    kv = [own_kv, along_row(own_kv, 1, 0), along_row(own_kv, -1, 0), along_row(own_kv, 2, 0)]
    kv += [along_row(piece, 0, 1) for piece in (after(own_kv, *kv[1:]), *kv[1:])]
    hidden = z_ring_first(hidden)
    out_weights = jnp.concatenate([after(top, own_kv), after(bottom, own_kv)], axis=0)
    out_weights = lax.all_gather(out_weights, "row", axis=0, tiled=False)
    attended = attend(kv, after(query, hidden[1], hidden[2]))
    attended = z_ring(attended)
    forth, back = (after(block, attended[1], attended[2]) for block in hidden[3:])
    hidden += z_ring_last(forth, back, FFL // 2)
    parts = out_part((2, 1, 3), bf16, hidden, attended, out_weights)
    parts = [along_col(part, step, 0) for part, step in zip(parts, (2, 1, 3))]
    summed = columns.astype(f32) + out_part((0,), f32, hidden, attended, out_weights)[0]
    for part in parts:
        summed = summed + part.astype(f32)
    return summed.astype(bf16).T


def solution(mesh):
    return jax.shard_map(
        on_device,
        mesh=mesh,
        in_specs=(
            P("row", "col"),
            P("col"),
            P("row", "col"),
            P("row", "col"),
            P("row", "col"),
            P("row", "col"),
            P("row", "col"),
            P("row", "col"),
            P("col", None),
            P("col", None),
        ),
        out_specs=P("row", "col"),
        check_vma=False,
    )
```

```python
import functools
import math

import jax
import jax.numpy as jnp
from jax import lax
from jax.experimental import pallas as pl
from jax.experimental.pallas import tpu as pltpu
from jax.sharding import PartitionSpec as P

D = 6144
HD = 128
NX, NY, NZ = 4, 4, 8
ROWS = 2 * NX
M = 512
BLOCK = D // (NY * NZ)
FIRST = 96
GAIN_ROWS = 16
PART1 = FIRST + GAIN_ROWS
PART2 = BLOCK - FIRST
DEEP = D // ROWS
FFL = 384
KV = 2 * HD
QU = HD + FFL
OUT_K = 512
DOWN_K = 1536
OUT_ROWS = DOWN_K + OUT_K
Y_OFF = (0, 1, 3, 2)
Z_OFF = (0, 1, 7, 2, 6, 3, 5, 4)
epsilon = 1e-06
f32, bf16 = jnp.float32, jnp.bfloat16
MIB = 1024 * 1024
ANY = pl.BlockSpec(memory_space=pl.ANY)
VMEM = pl.BlockSpec(memory_space=pltpu.VMEM)


def along_col(value, dy, dz):
    pairs = [
        (y * NZ + z, ((y + dy) % NY) * NZ + (z + dz) % NZ) for y in range(NY) for z in range(NZ)
    ]
    return lax.ppermute(value, "col", pairs)


def along_row(value, dx, dc):
    pairs = [
        (x * 2 + c, ((x + dx) % NX) * 2 + (c + dc) % 2) for x in range(NX) for c in range(2)
    ]
    return lax.ppermute(value, "row", pairs)


def z_ring(block, half=None):
    blocks = z_ring_first(block)
    return blocks + z_ring_last(blocks[3], blocks[4], half)


def z_ring_first(block):
    one, other = along_col(block, 0, 1), along_col(block, 0, -1)
    return [block, one, other, along_col(one, 0, 1), along_col(other, 0, -1)]


def z_ring_last(forth, back, half=None):
    forth, back = along_col(forth, 0, 1), along_col(back, 0, -1)
    if half is None:
        return [forth, back, along_col(forth, 0, 1)]
    return [forth, back, along_col(forth[:half], 0, 1), along_col(back[half:], 0, -1)]


def turn_over(block, shift):
    pairs = [
        (
            (x * 2 + c) * NY * NZ + y * NZ + z,
            (((x + y + shift) % NX) * 2 + c) * NY * NZ + x * NZ + z,
        )
        for x in range(NX)
        for c in range(2)
        for y in range(NY)
        for z in range(NZ)
    ]
    return lax.ppermute(block, ("row", "col"), pairs)


def position():
    col = lax.axis_index("col")
    return lax.div(col, NZ), lax.rem(col, NZ)


def back_from(index, offset, size):
    return lax.rem(index + (size - offset), size)


def start_all(copies, sems):
    started = []
    for number, (source, target) in enumerate(copies):
        copy = pltpu.make_async_copy(source, target, sems.at[number])
        copy.start()
        started.append(copy)
    return started


def head_norm(values, gain):
    gain = jnp.concatenate([jnp.broadcast_to(gain, (HD, HD)).T] * (M // HD), axis=1)
    average = jnp.mean(values, axis=0, keepdims=True)
    variance = jnp.mean(values * values, axis=0, keepdims=True) - average * average
    return (values - average) * lax.rsqrt(variance + epsilon) * gain


def piece_rows(refs, rows):
    spans = [(ref, place, 0, rows) for place, ref in enumerate(refs[:7])]
    if len(refs) == 8:
        return spans + [(refs[7], 7, 0, rows)]
    half = refs[7].shape[0]
    return spans + [(refs[7], 7, 0, half), (refs[8], 7, half, rows - half)]


def turn_kernel(k_weight, v_weight, q_weight, up_weight, out):
    begin = 0
    for weight in (k_weight, v_weight, q_weight, up_weight):
        for step in range(weight.shape[1] // HD):
            columns = weight[:, step * HD : (step + 1) * HD]
            out[begin : begin + HD, :] = columns.T
            begin += HD


def turn(*weights):
    return pl.pallas_call(
        turn_kernel,
        out_shape=jax.ShapeDtypeStruct((KV + QU, DEEP), bf16),
        in_specs=[VMEM] * 4,
        out_specs=VMEM,
        compiler_params=pltpu.CompilerParams(vmem_limit_bytes=56 * MIB),
        cost_estimate=pl.CostEstimate(flops=0, bytes_accessed=3 * 2**20, transcendentals=0),
        name="turn",
    )(*weights)


def add_rows(totals, rows):
    rows = rows.astype(f32).reshape(rows.shape[0] // 8, 8, M)
    return totals[0] + jnp.sum(rows, axis=0), totals[1] + jnp.sum(rows * rows, axis=0)


def early_sums_kernel(*refs):
    zero = jnp.zeros((8, M), f32)
    totals = zero, zero
    for piece in refs[:7]:
        for sub in range(NY):
            totals = add_rows(totals, piece[sub * PART1 : sub * PART1 + FIRST, :])
    for piece in refs[7:10]:
        for sub in range(NZ):
            totals = add_rows(totals, piece[sub * PART2 : (sub + 1) * PART2, :])
    refs[10][...], refs[11][...] = totals


def early_sums(pieces):
    return pl.pallas_call(
        early_sums_kernel,
        out_shape=(jax.ShapeDtypeStruct((8, M), f32),) * 2,
        in_specs=[VMEM] * 10,
        out_specs=(VMEM, VMEM),
        compiler_params=pltpu.CompilerParams(vmem_limit_bytes=16 * MIB),
        cost_estimate=pl.CostEstimate(
            flops=20 * D * M, bytes_accessed=6 * 2**20, transcendentals=0
        ),
        name="early_sums",
    )(*pieces)


def project_all_kernel(*refs):
    first, second = refs[:9], refs[9:14]
    sum_early, square_early, weights, k_gain, q_gain = refs[14:19]
    kv_out, q_out, hidden_out, held, normed, gains, gain_wide, w_held, sums, sems = refs[19:]
    y, z = position()
    copies = []
    for ref, place, begin, rows in piece_rows(first, NY * PART1):
        z_from = back_from(z, Z_OFF[place], NZ)
        for sub in range(rows // PART1):
            y_from = back_from(y, Y_OFF[begin // PART1 + sub], NY)
            block = y_from * NZ + z_from
            row = pl.multiple_of(block * BLOCK, 16)
            copies.append((ref.at[pl.ds(sub * PART1, FIRST)], held.at[pl.ds(row, FIRST)]))
            row = pl.multiple_of(block * GAIN_ROWS, 16)
            copies.append(
                (ref.at[pl.ds(sub * PART1 + FIRST, GAIN_ROWS)], gains.at[pl.ds(row, GAIN_ROWS)])
            )
    spans = [(second[0], 0, 0, 8), (second[1], 1, 0, 8), (second[2], 2, 0, 8)]
    spans += [(second[3], 3, 0, 4), (second[4], 3, 4, 4)]
    for ref, place, begin, count in spans:
        y_from = back_from(y, Y_OFF[place], NY)
        for sub in range(count):
            z_from = back_from(z, Z_OFF[begin + sub], NZ)
            row = pl.multiple_of((y_from * NZ + z_from) * BLOCK + FIRST, 16)
            copies.append((ref.at[pl.ds(sub * PART2, PART2)], held.at[pl.ds(row, PART2)]))
    for part in range(ROWS):
        copies.append((weights.at[part], w_held.at[part]))
    started = start_all(copies, sems)
    for copy in started[:-ROWS]:
        copy.wait()

    gain_rows = jnp.max(gains[:, :256].astype(f32).reshape(NY * NZ, GAIN_ROWS, 256), axis=1)
    gain_columns = gain_rows.T
    for block in range(NY * NZ):
        gain_wide[block * BLOCK : (block + 1) * BLOCK, :] = jnp.broadcast_to(
            gain_columns[:BLOCK, block : block + 1], (BLOCK, 128)
        )

    totals = sum_early[...], square_early[...]
    z_far, y_far = back_from(z, 4, NZ), back_from(y, 2, NY)
    late = [(y_from * NZ + z_far) * BLOCK for y_from in range(NY)]
    for row in late:
        totals = add_rows(totals, held[pl.ds(pl.multiple_of(row, 16), FIRST), :])
    late = [(y_far * NZ + z_from) * BLOCK + FIRST for z_from in range(NZ)]
    for row in late:
        totals = add_rows(totals, held[pl.ds(pl.multiple_of(row, 16), PART2), :])
    average = jnp.sum(totals[0], axis=0, keepdims=True) / D
    variance = jnp.sum(totals[1], axis=0, keepdims=True) / D - average * average
    scale = lax.rsqrt(variance + epsilon)
    for copy in started[-ROWS:]:
        copy.wait()

    chunk = 96
    for part in range(ROWS):
        for begin in range(part * DEEP, (part + 1) * DEEP, chunk):
            where = slice(begin, begin + chunk)
            gain = jnp.concatenate([gain_wide[where, :]] * 4, axis=1)
            rows = held[where, :].astype(f32)
            normed[where, :] = ((rows - average) * scale * gain).astype(bf16)
        product = jnp.dot(
            w_held[part], normed[part * DEEP : (part + 1) * DEEP, :], preferred_element_type=f32
        )
        if part == 0:
            sums[...] = product
        else:
            sums[...] += product
    kv_out[:HD, :] = head_norm(sums[:HD, :], k_gain[...]).astype(bf16)
    kv_out[HD:, :] = sums[HD:KV, :].astype(bf16)
    q_out[...] = head_norm(sums[KV : KV + HD, :], q_gain[...]).astype(bf16)
    hidden_out[...] = jax.nn.gelu(sums[KV + HD :, :]).astype(bf16)


def project_all(first, second, early, weights, k_gain, q_gain):
    copies = 64 + 32 + ROWS
    return pl.pallas_call(
        project_all_kernel,
        out_shape=(
            jax.ShapeDtypeStruct((KV, M), bf16),
            jax.ShapeDtypeStruct((HD, M), bf16),
            jax.ShapeDtypeStruct((FFL, M), bf16),
        ),
        in_specs=[ANY] * 14 + [VMEM] * 2 + [ANY] + [VMEM] * 2,
        out_specs=(VMEM, VMEM, VMEM),
        scratch_shapes=[
            pltpu.VMEM((D, M), bf16),
            pltpu.VMEM((D, M), bf16),
            pltpu.VMEM((NY * NZ * GAIN_ROWS, M), bf16),
            pltpu.VMEM((D, 128), f32),
            pltpu.VMEM((ROWS, KV + QU, DEEP), bf16),
            pltpu.VMEM((KV + QU, M), f32),
            pltpu.SemaphoreType.DMA((copies,)),
        ],
        compiler_params=pltpu.CompilerParams(vmem_limit_bytes=56 * MIB),
        cost_estimate=pl.CostEstimate(
            flops=2 * D * M * (KV + QU), bytes_accessed=18 * 2**20, transcendentals=FFL * M
        ),
        name="project_all",
    )(*first, *second, *early, weights, k_gain, q_gain)


def attend_kernel(*refs):
    pieces, query, out, scores = refs[:ROWS], refs[ROWS], refs[ROWS + 1], refs[ROWS + 2]
    largest = jnp.full((1, M), -jnp.inf, f32)
    for place, piece in enumerate(pieces):
        part = lax.dot_general(
            piece[:HD, :], query[...], (((0,), (0,)), ((), ())), preferred_element_type=f32
        ) * (1.0 / math.sqrt(HD))
        scores[place * M : (place + 1) * M, :] = part
        largest = jnp.maximum(largest, jnp.max(part, axis=0, keepdims=True))
    total = jnp.zeros((1, M), f32)
    for place in range(ROWS):
        part = jnp.exp(scores[place * M : (place + 1) * M, :] - largest)
        scores[place * M : (place + 1) * M, :] = part
        total = total + jnp.sum(part, axis=0, keepdims=True)
    share = 1.0 / total
    sums = jnp.zeros((HD, M), f32)
    for place, piece in enumerate(pieces):
        probs = (scores[place * M : (place + 1) * M, :] * share).astype(bf16)
        sums = sums + jnp.dot(piece[HD:, :], probs, preferred_element_type=f32)
    out[...] = sums.astype(bf16)


def attend(pieces, query):
    return pl.pallas_call(
        attend_kernel,
        out_shape=jax.ShapeDtypeStruct((HD, M), bf16),
        in_specs=[VMEM] * (ROWS + 1),
        out_specs=VMEM,
        scratch_shapes=[pltpu.VMEM((ROWS * M, M), f32)],
        compiler_params=pltpu.CompilerParams(vmem_limit_bytes=20 * MIB),
        cost_estimate=pl.CostEstimate(
            flops=20 * ROWS * M * M * HD, bytes_accessed=3 * 2**20, transcendentals=ROWS * M * M
        ),
        name="attend",
    )(*pieces, query)


def out_part_kernel(steps, *refs):
    hidden, attended, weights, outs = refs[:9], refs[9:17], refs[17], refs[18 : 18 + len(steps)]
    held, w_held, sems = refs[18 + len(steps) :]
    y, z = position()
    copies = []
    for pieces, rows, first_row in ((hidden, FFL, 0), (attended, HD, DOWN_K)):
        for ref, place, begin, count in piece_rows(pieces, rows):
            z_from = back_from(z, Z_OFF[place], NZ)
            row = lax.div(z_from, 4) * OUT_ROWS + lax.rem(z_from, 4) * rows + (first_row + begin)
            copies.append((ref, held.at[pl.ds(pl.multiple_of(row, 16), count)]))
    half = BLOCK // 2
    for place, step in enumerate(steps):
        for core in range(2):
            for part in range(2):
                source = weights.at[2 * lax.rem(2 * y + step + part, NX) + core]
                rows = pl.ds(part * half, half)
                copies.append((source.at[rows], w_held.at[2 * place + core].at[rows]))
    started = start_all(copies, sems)
    for copy in started[:17]:
        copy.wait()
    for place in range(len(steps)):
        for copy in started[17 + 4 * place : 21 + 4 * place]:
            copy.wait()
        total = jnp.dot(w_held[2 * place], held[:OUT_ROWS, :], preferred_element_type=f32)
        total = total + jnp.dot(
            w_held[2 * place + 1], held[OUT_ROWS:, :], preferred_element_type=f32
        )
        outs[place][...] = total.astype(outs[place].dtype)


def out_part(steps, kind, hidden, attended, weights):
    count = len(steps)
    return pl.pallas_call(
        functools.partial(out_part_kernel, steps),
        out_shape=(jax.ShapeDtypeStruct((BLOCK, M), kind),) * count,
        in_specs=[ANY] * 18,
        out_specs=(VMEM,) * count,
        scratch_shapes=[
            pltpu.VMEM((2 * OUT_ROWS, M), bf16),
            pltpu.VMEM((2 * count, BLOCK, OUT_ROWS), bf16),
            pltpu.SemaphoreType.DMA((17 + 4 * count,)),
        ],
        compiler_params=pltpu.CompilerParams(vmem_limit_bytes=56 * MIB),
        cost_estimate=pl.CostEstimate(
            flops=4 * count * BLOCK * M * OUT_ROWS,
            bytes_accessed=(4 + 2 * count) * 2**20,
            transcendentals=0,
        ),
        name="out_part",
    )(*hidden, *attended, weights)


def after(value, *others):
    return lax.optimization_barrier((value, *others))[0]


def on_device(
    tokens,
    ln_gain,
    q_weight,
    k_weight,
    v_weight,
    up_weight,
    out_weight,
    down_weight,
    q_gain,
    k_gain,
):
    columns = tokens.T
    in_weights = turn(k_weight, v_weight, q_weight, up_weight)
    in_weights = lax.all_gather(in_weights, "row", axis=0, tiled=False)

    gain_tile = jnp.broadcast_to(jnp.pad(ln_gain, (0, M - BLOCK))[None, :], (GAIN_ROWS, M))
    part1 = jnp.concatenate([columns[:FIRST], gain_tile], axis=0)
    part2 = z_ring(columns[FIRST:])
    part1 = jnp.concatenate(
        [part1, along_col(part1, 1, 0), along_col(part1, -1, 0), along_col(part1, 2, 0)], axis=0
    )
    first = z_ring(part1, NY * PART1 // 2)
    part2 = after(jnp.concatenate(part2, axis=0), first[1], first[2])
    forth, back = along_col(part2, 1, 0), along_col(part2, -1, 0)
    half = NZ * PART2 // 2
    top, bottom = after(forth[:half], first[5], first[6]), after(back[half:], first[5], first[6])
    second = [part2, forth, back, along_col(top, 1, 0), along_col(bottom, -1, 0)]

    early = early_sums(first[:7] + second[:3])
    out_weights = jnp.concatenate([down_weight.T, out_weight.T], axis=1)
    out_weights = after(out_weights, *first[7:], *second[3:], *early)
    half = BLOCK // 2
    out_weights = jnp.concatenate(
        [turn_over(out_weights[:half], 0), turn_over(out_weights[half:], 1)], axis=0
    )

    own_kv, query, hidden = project_all(first, second, early, in_weights, k_gain, q_gain)
    kv = [own_kv, along_row(own_kv, 1, 0), along_row(own_kv, -1, 0), along_row(own_kv, 2, 0)]
    kv += [along_row(piece, 0, 1) for piece in (after(own_kv, *kv[1:]), *kv[1:])]
    hidden = z_ring_first(hidden)
    out_weights = after(out_weights, own_kv)
    out_weights = lax.all_gather(out_weights, "row", axis=0, tiled=False)
    attended = attend(kv, after(query, hidden[1], hidden[2]))
    attended = z_ring(attended)
    forth, back = (after(block, attended[1], attended[2]) for block in hidden[3:])
    hidden += z_ring_last(forth, back, FFL // 2)
    parts = out_part((2, 1, 3), bf16, hidden, attended, out_weights)
    parts = [along_col(part, step, 0) for part, step in zip(parts, (2, 1, 3))]
    summed = columns.astype(f32) + out_part((0,), f32, hidden, attended, out_weights)[0]
    for part in parts:
        summed = summed + part.astype(f32)
    return summed.astype(bf16).T


def solution(mesh):
    return jax.shard_map(
        on_device,
        mesh=mesh,
        in_specs=(
            P("row", "col"),
            P("col"),
            P("row", "col"),
            P("row", "col"),
            P("row", "col"),
            P("row", "col"),
            P("row", "col"),
            P("row", "col"),
            P("col", None),
            P("col", None),
        ),
        out_specs=P("row", "col"),
        check_vma=False,
    )
```
